32 devices in a mesh: bx: 4 (over x, core), by: 4 (over z), bz: 2 (over y).
Axes of the slice: x: 2, y: 2, z: 4, core: 2. Of those that a mesh axis runs over, the one named last changes fastest.
Arguments:
- density: float32 [64, 512, 512], P('bz', 'bx', 'by'), may hold values from 0.2 to 2
- material: int32 [64, 512, 512], P('bz', 'bx', 'by'), may hold values from 0 to 255
- color_table: bfloat16 [3, 256], replicated, may hold values from 0.049804688 to 1
- extinction_table: bfloat16 [256], replicated, may hold values from 0.099609375 to 4
- order: int32 [4, 4, 2], P('bx', 'by'), may hold values from 0 to 1, as said below
Outputs:
- image: float32 [4, 512, 512], P(None, ('bx', 'bz'), 'by')
The draws below stay inside these ranges and needn't reach their ends.
Inputs may be any that keep to these rules, and one draw needn't show every extreme that they name: order[a, b, j] equals j XOR m for one number m of each brick column (a, b), the same for every slab j of that column.
All inputs are finite; a program needn't handle non-finite values.
Results may differ from the reference program's by a relative error of at most 0.0003.
Values sent between devices are 32-bit elements; how exact they have to be, the bound alone decides.
No kernel may reach another device: no remote copies, remote signals or barrier semaphores. Data moves between devices by JAX's collectives and lax.ppermute only.
A program may use at most 128 MiB of HBM per device.

```python
import math
import jax
import jax.numpy as jnp
from jax import lax

CX = 128
CY = 128
CZ = 32
TF_SIZE = 256
NX = 512
NY = 512
NZ = 64
N_BX = 4
N_BY = 4
N_BZ = 2


def draw_order(key, part):
    flip_mask = jax.random.randint(key, (N_BX, N_BY, 1), 0, N_BZ, dtype=jnp.int32)
    return jnp.bitwise_xor(jnp.arange(N_BZ, dtype=jnp.int32)[None, None, :], flip_mask)


def plant(drawn, key, low, largest):
    longest = drawn.shape.index(max(drawn.shape))
    spots = []
    for shift in (0, 1):
        where = [jax.random.randint(jax.random.fold_in(key, axis), (), 0, length) for axis, length in enumerate(drawn.shape)]
        where[longest] = (where[longest] + shift) % drawn.shape[longest]
        spots.append(tuple(where))
    return drawn.at[spots[0]].set(low).at[spots[1]].set(largest)


def levels(stream_key, shape, pieces, smallest, high):
    level, own = 1.0, jax.random.fold_in(stream_key, 6)
    for axis_at, shards_of in pieces:
        heights = jnp.exp(jax.random.uniform(jax.random.fold_in(own, axis_at), (shards_of,), jnp.float32, smallest / len(pieces), high / len(pieces)))
        level = level * jnp.repeat(heights, shape[axis_at] // shards_of).reshape([-1 if axis == axis_at else 1 for axis in range(len(shape))])
    return level


def setup_inputs(seed: int = 0) -> dict:
    splits = jax.random.split(jax.random.key(seed), 6)
    density = jnp.clip(jnp.exp(math.log(2.0) - 2.3025851 * jax.random.uniform(splits[0], (NZ, NX, NY), jnp.float32) ** levels(splits[0], (NZ, NX, NY), ((0, 2), (1, 4), (2, 4)), -0.2, 0.2)), 0.2, 2.0)
    material = plant(jax.random.randint(splits[1], (NZ, NX, NY), 0, TF_SIZE), jax.random.fold_in(splits[1], 1), 0, TF_SIZE - 1).astype(jnp.int32)
    color_table = jnp.clip(jax.random.uniform(splits[2], (3, TF_SIZE), jnp.float32, 0.049804688, 1.0), 0.049804688, 1.0).astype(jnp.bfloat16)
    extinction_table = jnp.clip(jnp.exp(jax.random.uniform(splits[3], (TF_SIZE,), jnp.float32, math.log(0.099609375), math.log(4.0))), 0.099609375, 4.0).astype(jnp.bfloat16)
    order = draw_order(jax.random.fold_in(splits[5], 71), 0)
    return {"density": density, "material": material, "color_table": color_table, "extinction_table": extinction_table, "order": order}


def stencil(far_below, below, above, far_above):
    return (8.0 * (above - below) - (far_above - far_below)) / 12.0

def plane_at(density, index):
    inside = jnp.logical_and(index >= 0, index < NZ)
    safe_index = jnp.clip(index, 0, NZ - 1).astype(jnp.int32)
    layer = lax.dynamic_index_in_dim(density, safe_index, 0, keepdims=False)
    return jnp.where(inside, layer, jnp.zeros_like(layer))

def sample_plane(density, material, color_table, extinction_table, index):
    layers = [plane_at(density, index + offset) for offset in (-2, -1, 0, 1, 2)]
    middle = layers[2]
    padded = jnp.pad(middle, 2)
    slope_z = stencil(layers[0], layers[1], layers[3], layers[4])
    slope_x = stencil(padded[0:NX, 2:-2], padded[1:NX + 1, 2:-2], padded[3:NX + 3, 2:-2], padded[4:NX + 4, 2:-2])
    slope_y = stencil(padded[2:-2, 0:NY], padded[2:-2, 1:NY + 1], padded[2:-2, 3:NY + 3], padded[2:-2, 4:NY + 4])
    magnitude = jnp.sqrt(slope_x * slope_x + slope_y * slope_y + slope_z * slope_z)
    facing = jnp.abs(0.48 * slope_x + 0.6 * slope_y + 0.64 * slope_z)
    shading = 0.1 + 0.9 * facing / jnp.maximum(magnitude, 0.5)
    labels = lax.dynamic_index_in_dim(material, index.astype(jnp.int32), 0, keepdims=False)
    colors = color_table.astype(jnp.float32)[:, labels]
    extinction = extinction_table.astype(jnp.float32)[labels]
    optical = 3.0 * extinction * middle / NZ
    opacity = 1.0 - jnp.exp(-optical)
    emission = colors * (shading * opacity)[None]
    return (emission, optical)

def slab_partial(density, material, color_table, extinction_table, slab, backward):

    def visit(carry, local_plane):
        color_sum, depth_sum = carry
        index = (jnp.int32(slab * CZ) + local_plane).astype(jnp.int32)
        emission, optical = sample_plane(density, material, color_table, extinction_table, index)
        color_sum = color_sum + emission * jnp.exp(-depth_sum)[None]
        return ((color_sum, depth_sum + optical), None)
    start_state = (jnp.zeros((3, NX, NY), jnp.float32), jnp.zeros((NX, NY), jnp.float32))
    (color_sum, depth_sum), _ = lax.scan(visit, start_state, jnp.arange(CZ, dtype=jnp.int32), reverse=backward)
    return (color_sum, depth_sum)

def reference(density, material, color_table, extinction_table, order):
    order_pixel = jnp.repeat(jnp.repeat(order, CX, axis=0), CY, axis=1)
    reverse_pixel = order_pixel[:, :, 0] > order_pixel[:, :, N_BZ - 1]
    slab_colors = []
    slab_depths = []
    for slab in range(N_BZ):
        forward_color, forward_depth = slab_partial(density, material, color_table, extinction_table, slab, False)
        backward_color, backward_depth = slab_partial(density, material, color_table, extinction_table, slab, True)
        slab_colors.append(jnp.where(reverse_pixel[None], backward_color, forward_color))
        slab_depths.append(jnp.where(reverse_pixel, backward_depth, forward_depth))
    color_total = jnp.zeros((3, NX, NY), jnp.float32)
    depth_total = jnp.zeros((NX, NY), jnp.float32)
    for slab in range(N_BZ):
        ahead = jnp.zeros((NX, NY), jnp.float32)
        for other in range(N_BZ):
            before = order_pixel[:, :, other] < order_pixel[:, :, slab]
            ahead = ahead + jnp.where(before, slab_depths[other], 0.0)
        color_total = color_total + slab_colors[slab] * jnp.exp(-ahead)[None]
        depth_total = depth_total + slab_depths[slab]
    return jnp.concatenate([color_total, (1.0 - jnp.exp(-depth_total))[None]], axis=0)
```

```python
import functools
import math

import jax
import jax.numpy as jnp
from jax import lax
from jax.experimental import pallas as pl
from jax.experimental.pallas import tpu as pltpu
from jax.sharding import PartitionSpec as P

LANES = 128
SUBLANES = 8
PAD = 8
REACH = 2
COLOR_UNIT = 4096.0
EXTINCTION_UNIT = 2048.0
VMEM_LIMIT = 48 * 2**20

VMEM = pl.BlockSpec(memory_space=pltpu.VMEM)
SMEM = pl.BlockSpec(memory_space=pltpu.SMEM)
ANY = pl.BlockSpec(memory_space=pl.ANY)


def lane_index():
    return lax.broadcasted_iota(jnp.int32, (SUBLANES, LANES), 1)


def is_odd(axis):
    return jnp.bitwise_and(lax.axis_index(axis), 1) == 1


def swaps(count):
    first = [(i, i ^ 1) for i in range(count)]
    second = [(i, i + 1 if i % 2 else i - 1) for i in range(1, count - 1)]
    return first, second


def faces_kernel(counts, density, padded, y_out, xa, xb, za, zb, arrived):
    planes, rows, _ = density.shape
    parts = arrived.shape[0]
    step = rows // parts
    copies = [
        pltpu.make_async_copy(
            density.at[:, pl.ds(k * step, step), :],
            padded.at[pl.ds(REACH, planes), pl.ds(PAD + k * step, step), :],
            arrived.at[k],
        )
        for k in range(parts)
    ]
    for copy in copies:
        copy.start()
    slot = jnp.right_shift(lane_index(), 2)
    for k in range(parts):
        copies[k].wait()
        for tile in range(step // SUBLANES):
            row = k * step + tile * SUBLANES
            packed = jnp.zeros((SUBLANES, LANES), jnp.float32)
            for z in range(planes):
                plane = padded[REACH + z, PAD + row : PAD + row + SUBLANES, :]
                packed = jnp.where(slot == z, pltpu.roll(plane, (4 * z + REACH) % LANES, 1), packed)
            y_out[row : row + SUBLANES, :] = packed
    odd_x, odd_z = is_odd("bx"), is_odd("bz")
    low_x, high_x = PAD, PAD + rows - REACH
    low_z, high_z = REACH, planes
    for out, start in ((xa, jnp.where(odd_x, low_x, high_x)), (xb, jnp.where(odd_x, high_x, low_x))):
        for z in range(planes):
            out[REACH * z : REACH * (z + 1), :] = padded[REACH + z, pl.ds(start, REACH), :]
    for out, start in ((za, jnp.where(odd_z, low_z, high_z)), (zb, jnp.where(odd_z, high_z, low_z))):
        if out is zb and counts["bz"] == 2:
            continue
        for layer in range(REACH):
            out[layer] = padded[start + layer, PAD : PAD + rows, :]
    if counts["bz"] == 2:
        zb[...] = jnp.zeros(zb.shape, jnp.float32)


def faces(density, counts):
    planes, rows, cols = density.shape
    shape = lambda *dims: jax.ShapeDtypeStruct(dims, jnp.float32)
    z_rows = rows if counts["bz"] > 2 else SUBLANES
    return pl.pallas_call(
        functools.partial(faces_kernel, counts),
        out_shape=(
            shape(planes + 2 * REACH, rows + 2 * PAD, cols),
            shape(rows, LANES),
            shape(REACH * planes, cols),
            shape(REACH * planes, cols),
            shape(REACH, rows, cols),
            shape(REACH, z_rows, cols),
        ),
        in_specs=[ANY],
        out_specs=(VMEM,) * 6,
        scratch_shapes=[pltpu.SemaphoreType.DMA((4,))],
        compiler_params=pltpu.CompilerParams(vmem_limit_bytes=VMEM_LIMIT),
        name="faces",
    )(density)


def local_kernel(total_planes, order, padded, material, colors, extinction, lit, slope_y, through):
    planes, rows, _ = material.shape
    slabs = lax.axis_size("bz")
    backward = order[0, 0, 0] > order[0, 0, slabs - 1]
    k = jnp.bitwise_and(lax.broadcasted_iota(jnp.int32, (2 * LANES, LANES), 0), LANES - 1)
    gap = k - lax.broadcasted_iota(jnp.int32, (2 * LANES, LANES), 1)
    band = jnp.where(gap == 1, 8.0, jnp.where(gap == -1, -8.0, 0.0))
    band = band + jnp.where(gap == 2, -1.0, jnp.where(gap == -2, 1.0, 0.0))
    band = band.astype(jnp.bfloat16)

    def derive(step, carry):
        for z in (2 * step, 2 * step + 1):
            plane = padded[REACH + z, PAD : PAD + rows, :]
            coarse = plane.astype(jnp.bfloat16)
            fine = (plane - coarse.astype(jnp.float32)).astype(jnp.bfloat16)
            slope_y[z] = jnp.dot(
                jnp.concatenate([coarse, fine], axis=1), band, preferred_element_type=jnp.float32
            )
        return carry

    lax.fori_loop(0, planes // 2, derive, 0)

    color = (colors[...].astype(jnp.float32) * COLOR_UNIT).astype(jnp.int32)
    dense = (extinction[...].astype(jnp.float32) * EXTINCTION_UNIT).astype(jnp.int32)

    def halves(row):
        return [
            jnp.broadcast_to(row[:, start : start + LANES], (SUBLANES, LANES))
            for start in (0, LANES)
        ]

    red_green = halves(color[0:1] * 65536 + color[1:2])
    blue_dense = halves(color[2:3] * 65536 + dense)
    scale = -3.0 * math.log2(math.e) / (EXTINCTION_UNIT * total_planes)

    def take(table, low, upper):
        found = [jnp.take_along_axis(t, low, axis=1, mode="promise_in_bounds") for t in table]
        return jnp.where(upper, found[1], found[0])

    def tile(index, carry):
        row = pl.multiple_of(index * SUBLANES, SUBLANES)
        clear = jnp.ones((SUBLANES, LANES), jnp.float32)
        for visit in range(planes):
            z = jnp.where(backward, planes - 1 - visit, visit)
            density = padded[REACH + z, pl.ds(PAD + row, SUBLANES), :]
            label = material[z, pl.ds(row, SUBLANES), :]
            low = jnp.bitwise_and(label, LANES - 1)
            upper = label >= LANES
            rg = take(red_green, low, upper)
            be = take(blue_dense, low, upper)
            extinct = jnp.bitwise_and(be, 65535).astype(jnp.float32)
            after = clear * jnp.exp2(extinct * (density * scale))
            stopped = clear - after
            lit[0, z, pl.ds(row, SUBLANES), :] = stopped * jnp.right_shift(rg, 16).astype(jnp.float32)
            lit[1, z, pl.ds(row, SUBLANES), :] = stopped * jnp.bitwise_and(rg, 65535).astype(jnp.float32)
            lit[2, z, pl.ds(row, SUBLANES), :] = stopped * jnp.right_shift(be, 16).astype(jnp.float32)
            clear = after
        through[pl.ds(row, SUBLANES), :] = clear
        return carry

    lax.fori_loop(0, rows // SUBLANES, tile, 0)


def local(order, padded, material, colors, extinction, total_planes):
    planes, rows, cols = material.shape
    shape = lambda *dims: jax.ShapeDtypeStruct(dims, jnp.float32)
    return pl.pallas_call(
        functools.partial(local_kernel, total_planes),
        out_shape=(shape(3, planes, rows, cols), shape(planes, rows, cols), shape(rows, cols)),
        in_specs=[SMEM] + [VMEM] * 4,
        out_specs=(VMEM,) * 3,
        compiler_params=pltpu.CompilerParams(vmem_limit_bytes=VMEM_LIMIT),
        cost_estimate=pl.CostEstimate(flops=20 * planes * rows * cols, bytes_accessed=2**22, transcendentals=planes * rows * cols),
        name="local",
    )(order, padded, material, colors, extinction)


def put_halo(padded, xa, xb, za, zb, ya, yb, edge, planes, rows):
    odd_x, odd_y, odd_z = is_odd("bx"), is_odd("by"), is_odd("bz")
    for z in range(planes):
        first, second = xa[REACH * z : REACH * (z + 1), :], xb[REACH * z : REACH * (z + 1), :]
        padded[REACH + z, PAD - REACH : PAD, :] = jnp.where(odd_x, first, second)
        padded[REACH + z, PAD + rows : PAD + rows + REACH, :] = jnp.where(odd_x, second, first)
    for layer in range(REACH):
        first = za[layer]
        second = zb[layer] if zb.shape == za.shape else jnp.zeros_like(first)
        padded[layer, PAD : PAD + rows, :] = jnp.where(odd_z, first, second)
        padded[REACH + planes + layer, PAD : PAD + rows, :] = jnp.where(odd_z, second, first)
    side = jnp.bitwise_and(lane_index(), 3)
    for row in range(0, rows, SUBLANES):
        first, second = ya[row : row + SUBLANES, :], yb[row : row + SUBLANES, :]
        near = jnp.where((side < 2) == odd_y, first, second)
        ahead1, ahead2 = pltpu.roll(near, LANES - 1, 1), pltpu.roll(near, LANES - 2, 1)
        behind1, behind2 = pltpu.roll(near, 1, 1), pltpu.roll(near, 2, 1)
        edge[row : row + SUBLANES, :] = jnp.where(
            side == 0,
            -ahead2,
            jnp.where(
                side == 1,
                8.0 * ahead1 - ahead2,
                jnp.where(side == 2, behind2 - 8.0 * behind1, behind2),
            ),
        )


def shade_kernel(padded_in, xa, xb, za, zb, ya, yb, lit, slope_y, through, padded, give, keep, edge):
    _, planes, rows, _ = lit.shape
    del padded_in
    put_halo(padded, xa, xb, za, zb, ya, yb, edge, planes, rows)
    slabs = lax.axis_size("bz")
    block_rows = rows // slabs
    my_half = jnp.bitwise_and(lax.axis_index("bz"), 1)
    lane = lane_index()
    at_edge = jnp.logical_or(lane < REACH, lane >= LANES - REACH)
    for out, half in ((give, 1 - my_half), (keep, my_half)):

        def tile(index, carry, out=out, half=half):
            to = pl.multiple_of(index * SUBLANES, SUBLANES)
            group = lax.div(to, block_rows)
            row = (group + half) * block_rows + to
            row = pl.multiple_of(row, SUBLANES)
            beside = edge[pl.ds(row, SUBLANES), :]
            sums = [jnp.zeros((SUBLANES, LANES), jnp.float32) for _ in range(3)]
            for z in range(planes):
                at = lambda dz, dx: padded[REACH + z + dz, pl.ds(PAD + row + dx, SUBLANES), :]
                sz = 8.0 * (at(1, 0) - at(-1, 0)) - (at(2, 0) - at(-2, 0))
                sx = 8.0 * (at(0, 1) - at(0, -1)) - (at(0, 2) - at(0, -2))
                outer = pltpu.roll(beside, (-4 * z - REACH) % LANES, 1)
                sy = slope_y[z, pl.ds(row, SUBLANES), :] + jnp.where(at_edge, outer, 0.0)
                size = sx * sx + sy * sy + sz * sz
                facing = jnp.abs(0.432 * sx + 0.54 * sy + 0.576 * sz)
                shading = 0.1 + facing * lax.rsqrt(jnp.maximum(size, 36.0))
                for c in range(3):
                    sums[c] = sums[c] + shading * lit[c, z, pl.ds(row, SUBLANES), :]
            for c in range(3):
                out[c, pl.ds(to, SUBLANES), :] = sums[c] * (1.0 / COLOR_UNIT)
            out[3, pl.ds(to, SUBLANES), :] = through[pl.ds(row, SUBLANES), :]
            return carry

        lax.fori_loop(0, rows // 2 // SUBLANES, tile, 0)


def shade(padded, halos, lit, slope_y, through):
    _, planes, rows, cols = lit.shape
    shape = lambda *dims: jax.ShapeDtypeStruct(dims, jnp.float32)
    return pl.pallas_call(
        shade_kernel,
        out_shape=(
            shape(*padded.shape),
            shape(4, rows // 2, cols),
            shape(4, rows // 2, cols),
        ),
        in_specs=[VMEM] * 10,
        out_specs=(VMEM,) * 3,
        scratch_shapes=[pltpu.VMEM((rows, LANES), jnp.float32)],
        input_output_aliases={0: 0},
        compiler_params=pltpu.CompilerParams(vmem_limit_bytes=VMEM_LIMIT),
        name="shade",
    )(padded, *halos, lit, slope_y, through)


def blend_kernel(bit, last, order, mine, other, out):
    rank = jnp.bitwise_xor(lax.axis_index("bz"), order[0, 0, 0])
    in_front = jnp.bitwise_and(jnp.right_shift(rank, bit), 1) == 0
    clear = jnp.where(in_front, mine[3], other[3])
    for c in range(3):
        front = jnp.where(in_front, mine[c], other[c])
        back = jnp.where(in_front, other[c], mine[c])
        out[c] = front + clear * back
    product = mine[3] * other[3]
    out[3] = 1.0 - product if last else product


def blend(order, mine, other, bit, last):
    return pl.pallas_call(
        functools.partial(blend_kernel, bit, last),
        out_shape=jax.ShapeDtypeStruct(mine.shape, jnp.float32),
        in_specs=[SMEM, VMEM, VMEM],
        out_specs=VMEM,
        compiler_params=pltpu.CompilerParams(vmem_limit_bytes=VMEM_LIMIT),
        name="blend",
    )(order, mine, other)


def shards(density, material, color_table, extinction_table, order):
    planes, rows, cols = density.shape
    counts = {axis: lax.axis_size(axis) for axis in ("bx", "by", "bz")}
    slabs = counts["bz"]
    padded, y_own, xa, xb, za, zb = faces(density, counts)
    pairs = {axis: swaps(counts[axis]) for axis in counts}
    xa = lax.ppermute(xa, "bx", pairs["bx"][0])
    xb = lax.ppermute(xb, "bx", pairs["bx"][1])
    za = lax.ppermute(za, "bz", pairs["bz"][0])
    if slabs > 2:
        zb = lax.ppermute(zb, "bz", pairs["bz"][1])
    ya = lax.ppermute(y_own, "by", pairs["by"][0])
    yb = lax.ppermute(y_own, "by", pairs["by"][1])
    lit, slope_y, through = local(
        order, padded, material, color_table, extinction_table.reshape(1, -1), planes * slabs
    )
    _, give, keep = shade(padded, (xa, xb, za, zb, ya, yb), lit, slope_y, through)
    block_rows = rows // slabs
    levels = slabs.bit_length() - 1
    my_slab = lax.axis_index("bz")
    for bit in range(levels):
        flip = [(i, i ^ (1 << bit)) for i in range(slabs)]
        received = lax.ppermute(give, "bz", flip)
        holding = blend(order, keep, received, bit, bit == levels - 1)
        if bit < levels - 1:
            paired = holding.reshape(4, -1, 2, block_rows, cols)
            half = jnp.bitwise_and(jnp.right_shift(my_slab, bit + 1), 1)
            take = lambda which: lax.dynamic_index_in_dim(paired, which, 2, keepdims=False)
            keep, give = (take(which).reshape(4, -1, cols) for which in (half, 1 - half))
    return holding


def solution(mesh):
    placed = (P("bz", "bx", "by"), P("bz", "bx", "by"), P(), P(), P("bx", "by", None))
    return jax.shard_map(
        shards, mesh=mesh, in_specs=placed, out_specs=P(None, ("bx", "bz"), "by"), check_vma=False
    )
```

```python
import functools
import math

import jax
import jax.numpy as jnp
from jax import lax
from jax.experimental import pallas as pl
from jax.experimental.pallas import tpu as pltpu
from jax.sharding import PartitionSpec as P

LANES = 128
SUBLANES = 8
PAD = 8
REACH = 2
COLOR_UNIT = 4096.0
EXTINCTION_UNIT = 2048.0
VMEM_LIMIT = 12 * 2**20
FACES_LIMIT = 58 * 2**20

VMEM = pl.BlockSpec(memory_space=pltpu.VMEM)
HBM = pl.BlockSpec(memory_space=pltpu.HBM)


def lane_index():
    return lax.broadcasted_iota(jnp.int32, (SUBLANES, LANES), 1)


def is_odd(axis):
    return jnp.bitwise_and(lax.axis_index(axis), 1) == 1


def swaps(count):
    first = [(i, i ^ 1) for i in range(count)]
    second = [(i, i + 1 if i % 2 else i - 1) for i in range(1, count - 1)]
    return first, second


def faces_kernel(counts, order, density, colors, extinction, padded, y_out, xa, xb, za, zb, tables, flags, place, hues, thick, arrived):
    planes, rows, _ = density.shape
    parts = arrived.shape[0] - 3
    step = rows // parts
    copies = [
        pltpu.make_async_copy(
            density.at[:, pl.ds(k * step, step), :],
            padded.at[pl.ds(REACH, planes), pl.ds(PAD + k * step, step), :],
            arrived.at[k],
        )
        for k in range(parts)
    ]
    small = [
        pltpu.make_async_copy(source, target, arrived.at[parts + k])
        for k, (source, target) in enumerate(((order, place), (colors, hues), (extinction, thick)))
    ]
    for copy in copies + small:
        copy.start()
    slot = jnp.right_shift(lane_index(), 2)
    for k in range(parts):
        copies[k].wait()
        for tile in range(step // SUBLANES):
            row = k * step + tile * SUBLANES
            packed = jnp.zeros((SUBLANES, LANES), jnp.float32)
            for z in range(planes):
                plane = padded[REACH + z, PAD + row : PAD + row + SUBLANES, :]
                packed = jnp.where(slot == z, pltpu.roll(plane, (4 * z + REACH) % LANES, 1), packed)
            y_out[row : row + SUBLANES, :] = packed
    odd_x, odd_z = is_odd("bx"), is_odd("bz")
    low_x, high_x = PAD, PAD + rows - REACH
    low_z, high_z = REACH, planes
    for out, start in ((xa, jnp.where(odd_x, low_x, high_x)), (xb, jnp.where(odd_x, high_x, low_x))):
        for z in range(planes):
            out[REACH * z : REACH * (z + 1), :] = padded[REACH + z, pl.ds(start, REACH), :]
    for out, start in ((za, jnp.where(odd_z, low_z, high_z)), (zb, jnp.where(odd_z, high_z, low_z))):
        if out is zb and counts["bz"] == 2:
            continue
        for layer in range(REACH):
            out[layer] = padded[start + layer, PAD : PAD + rows, :]
    if counts["bz"] == 2:
        zb[...] = jnp.zeros(zb.shape, jnp.float32)
    for copy in small:
        copy.wait()
    slabs = counts["bz"]
    backward = (place[0, 0, 0] > place[0, 0, slabs - 1]).astype(jnp.float32)
    rank = jnp.bitwise_xor(lax.axis_index("bz"), place[0, 0, 0])
    flags[0] = jnp.full((SUBLANES, LANES), backward, jnp.float32)
    for bit in range(slabs.bit_length() - 1):
        behind = jnp.bitwise_and(jnp.right_shift(rank, bit), 1).astype(jnp.float32)
        flags[1 + bit] = jnp.full((SUBLANES, LANES), behind, jnp.float32)
    color = (hues[...].astype(jnp.float32) * COLOR_UNIT).astype(jnp.int32)
    dense = (thick[...].astype(jnp.float32) * EXTINCTION_UNIT).astype(jnp.int32)
    for k, table in enumerate((color[0:1] * 65536 + color[1:2], color[2:3] * 65536 + dense)):
        for part in range(2):
            tables[2 * k + part] = jnp.broadcast_to(
                table[:, part * LANES : (part + 1) * LANES], (SUBLANES, LANES)
            )


def faces(order, density, colors, extinction, counts):
    planes, rows, cols = density.shape
    shape = lambda *dims: jax.ShapeDtypeStruct(dims, jnp.float32)
    z_rows = rows if counts["bz"] > 2 else SUBLANES
    return pl.pallas_call(
        functools.partial(faces_kernel, counts),
        out_shape=(
            shape(planes + 2 * REACH, rows + 2 * PAD, cols),
            shape(rows, LANES),
            shape(REACH * planes, cols),
            shape(REACH * planes, cols),
            shape(REACH, rows, cols),
            shape(REACH, z_rows, cols),
            jax.ShapeDtypeStruct((4, SUBLANES, LANES), jnp.int32),
            shape(counts["bz"].bit_length(), SUBLANES, LANES),
        ),
        in_specs=[HBM] * 4,
        out_specs=(VMEM,) * 8,
        scratch_shapes=[
            pltpu.SMEM(order.shape, jnp.int32),
            pltpu.VMEM(colors.shape, colors.dtype),
            pltpu.VMEM(extinction.shape, extinction.dtype),
            pltpu.SemaphoreType.DMA((7,)),
        ],
        compiler_params=pltpu.CompilerParams(vmem_limit_bytes=FACES_LIMIT),
        name="faces",
    )(order, density, colors, extinction)


def local_kernel(total_planes, padded, material, tables, flags, lit, slope_y, through):
    planes, rows, _ = material.shape
    backward = jnp.max(flags[0]) > 0.5
    k = jnp.bitwise_and(lax.broadcasted_iota(jnp.int32, (2 * LANES, LANES), 0), LANES - 1)
    gap = k - lax.broadcasted_iota(jnp.int32, (2 * LANES, LANES), 1)
    band = jnp.where(gap == 1, 8.0, jnp.where(gap == -1, -8.0, 0.0))
    band = band + jnp.where(gap == 2, -1.0, jnp.where(gap == -2, 1.0, 0.0))
    band = band.astype(jnp.bfloat16)
    scale = -3.0 * math.log2(math.e) / (EXTINCTION_UNIT * total_planes)

    def take(first, low, upper):
        found = [
            jnp.take_along_axis(tables[first + k], low, axis=1, mode="promise_in_bounds")
            for k in range(2)
        ]
        return jnp.where(upper, found[1], found[0])

    def tile(index, carry):
        top = pl.multiple_of(index * 2 * SUBLANES, 2 * SUBLANES)
        coarse, fine = [], []
        for z in range(planes):
            plane = padded[REACH + z, pl.ds(PAD + top, 2 * SUBLANES), :]
            rounded = plane.astype(jnp.bfloat16)
            coarse.append(rounded)
            fine.append((plane - rounded.astype(jnp.float32)).astype(jnp.bfloat16))
        both = jnp.concatenate(
            [jnp.concatenate(coarse, axis=0), jnp.concatenate(fine, axis=0)], axis=1
        )
        slopes = jnp.dot(both, band, preferred_element_type=jnp.float32)
        for z in range(planes):
            slope_y[z, pl.ds(top, 2 * SUBLANES), :] = slopes[2 * SUBLANES * z : 2 * SUBLANES * (z + 1)]
        for part in range(2):
            row = pl.multiple_of(top + part * SUBLANES, SUBLANES)
            clear = jnp.ones((SUBLANES, LANES), jnp.float32)
            for visit in range(planes):
                z = jnp.where(backward, planes - 1 - visit, visit)
                density = padded[REACH + z, pl.ds(PAD + row, SUBLANES), :]
                label = material[z, pl.ds(row, SUBLANES), :]
                low = jnp.bitwise_and(label, LANES - 1)
                upper = label >= LANES
                rg = take(0, low, upper)
                be = take(2, low, upper)
                extinct = jnp.bitwise_and(be, 65535).astype(jnp.float32)
                after = clear * jnp.exp2(extinct * (density * scale))
                stopped = clear - after
                here = (z, pl.ds(row, SUBLANES), slice(None))
                lit[(0, *here)] = stopped * jnp.right_shift(rg, 16).astype(jnp.float32)
                lit[(1, *here)] = stopped * jnp.bitwise_and(rg, 65535).astype(jnp.float32)
                lit[(2, *here)] = stopped * jnp.right_shift(be, 16).astype(jnp.float32)
                clear = after
            through[pl.ds(row, SUBLANES), :] = clear
        return carry

    lax.fori_loop(0, rows // SUBLANES // 2, tile, 0)


def local(padded, material, tables, flags, total_planes):
    planes, rows, cols = material.shape
    shape = lambda *dims: jax.ShapeDtypeStruct(dims, jnp.float32)
    return pl.pallas_call(
        functools.partial(local_kernel, total_planes),
        out_shape=(shape(3, planes, rows, cols), shape(planes, rows, cols), shape(rows, cols)),
        in_specs=[VMEM] * 4,
        out_specs=(VMEM,) * 3,
        compiler_params=pltpu.CompilerParams(vmem_limit_bytes=VMEM_LIMIT),
        cost_estimate=pl.CostEstimate(
            flops=20 * planes * rows * cols,
            bytes_accessed=2**22,
            transcendentals=planes * rows * cols,
        ),
        name="local",
    )(padded, material, tables, flags)


def put_halo(padded, xa, xb, za, zb, ya, yb, edge, planes, rows):
    odd_x, odd_y, odd_z = is_odd("bx"), is_odd("by"), is_odd("bz")
    for z in range(planes):
        first, second = xa[REACH * z : REACH * (z + 1), :], xb[REACH * z : REACH * (z + 1), :]
        padded[REACH + z, PAD - REACH : PAD, :] = jnp.where(odd_x, first, second)
        padded[REACH + z, PAD + rows : PAD + rows + REACH, :] = jnp.where(odd_x, second, first)
    for layer in range(REACH):
        first = za[layer]
        second = zb[layer] if zb.shape == za.shape else jnp.zeros_like(first)
        padded[layer, PAD : PAD + rows, :] = jnp.where(odd_z, first, second)
        padded[REACH + planes + layer, PAD : PAD + rows, :] = jnp.where(odd_z, second, first)
    side = jnp.bitwise_and(lane_index(), 3)
    for row in range(0, rows, SUBLANES):
        first, second = ya[row : row + SUBLANES, :], yb[row : row + SUBLANES, :]
        near = jnp.where((side < 2) == odd_y, first, second)
        ahead1, ahead2 = pltpu.roll(near, LANES - 1, 1), pltpu.roll(near, LANES - 2, 1)
        behind1, behind2 = pltpu.roll(near, 1, 1), pltpu.roll(near, 2, 1)
        edge[row : row + SUBLANES, :] = jnp.where(
            side == 0,
            -ahead2,
            jnp.where(
                side == 1,
                8.0 * ahead1 - ahead2,
                jnp.where(side == 2, behind2 - 8.0 * behind1, behind2),
            ),
        )


def shade_half(padded, edge, lit, slope_y, through, out, giving):
    _, planes, rows, _ = lit.shape
    block_rows = rows // lax.axis_size("bz")
    half = jnp.bitwise_and(lax.axis_index("bz") + (1 if giving else 0), 1)
    lane = lane_index()
    at_edge = jnp.logical_or(lane < REACH, lane >= LANES - REACH)

    def pair(index, carry):
        for part in range(2):
            to = pl.multiple_of((2 * index + part) * SUBLANES, SUBLANES)
            group = lax.div(to, block_rows)
            row = pl.multiple_of((group + half) * block_rows + to, SUBLANES)
            beside = edge[pl.ds(row, SUBLANES), :]
            sums = [jnp.zeros((SUBLANES, LANES), jnp.float32) for _ in range(3)]
            for z in range(planes):
                at = lambda dz, dx: padded[REACH + z + dz, pl.ds(PAD + row + dx, SUBLANES), :]
                sz = 8.0 * (at(1, 0) - at(-1, 0)) - (at(2, 0) - at(-2, 0))
                sx = 8.0 * (at(0, 1) - at(0, -1)) - (at(0, 2) - at(0, -2))
                outer = pltpu.roll(beside, (-4 * z - REACH) % LANES, 1)
                sy = slope_y[z, pl.ds(row, SUBLANES), :] + jnp.where(at_edge, outer, 0.0)
                size = sx * sx + sy * sy + sz * sz
                facing = jnp.abs(0.432 * sx + 0.54 * sy + 0.576 * sz)
                shading = 0.1 + facing * lax.rsqrt(jnp.maximum(size, 36.0))
                for c in range(3):
                    sums[c] = sums[c] + shading * lit[c, z, pl.ds(row, SUBLANES), :]
            for c in range(3):
                out[c, pl.ds(to, SUBLANES), :] = sums[c] * (1.0 / COLOR_UNIT)
            out[3, pl.ds(to, SUBLANES), :] = through[pl.ds(row, SUBLANES), :]
        return carry

    lax.fori_loop(0, rows // 4 // SUBLANES, pair, 0)


def shade_give_kernel(padded_in, xa, xb, za, zb, ya, yb, lit, slope_y, through, padded, edge, give):
    _, planes, rows, _ = lit.shape
    del padded_in
    put_halo(padded, xa, xb, za, zb, ya, yb, edge, planes, rows)
    shade_half(padded, edge, lit, slope_y, through, give, True)


def shade_keep_kernel(padded, edge, lit, slope_y, through, keep):
    shade_half(padded, edge, lit, slope_y, through, keep, False)


def shade_give(padded, halos, lit, slope_y, through):
    _, _, rows, cols = lit.shape
    shape = lambda *dims: jax.ShapeDtypeStruct(dims, jnp.float32)
    return pl.pallas_call(
        shade_give_kernel,
        out_shape=(shape(*padded.shape), shape(rows, LANES), shape(4, rows // 2, cols)),
        in_specs=[VMEM] * 10,
        out_specs=(VMEM,) * 3,
        input_output_aliases={0: 0},
        compiler_params=pltpu.CompilerParams(vmem_limit_bytes=VMEM_LIMIT),
        name="shade_give",
    )(padded, *halos, lit, slope_y, through)


def shade_keep(padded, edge, lit, slope_y, through):
    _, planes, rows, cols = lit.shape
    return pl.pallas_call(
        shade_keep_kernel,
        out_shape=jax.ShapeDtypeStruct((4, rows // 2, cols), jnp.float32),
        in_specs=[VMEM] * 5,
        out_specs=VMEM,
        compiler_params=pltpu.CompilerParams(vmem_limit_bytes=VMEM_LIMIT),
        cost_estimate=pl.CostEstimate(
            flops=20 * planes * rows * cols, bytes_accessed=2**22, transcendentals=0
        ),
        name="shade_keep",
    )(padded, edge, lit, slope_y, through)


def blend_kernel(bit, last, flags, mine, other, out):
    clear_mine, clear_other = mine[3], other[3]
    behind = jnp.broadcast_to(flags[1 + bit, 0:1, :], clear_mine.shape) > 0.5
    clear = jnp.where(behind, clear_other, clear_mine)
    for c in range(3):
        front = jnp.where(behind, other[c], mine[c])
        back = jnp.where(behind, mine[c], other[c])
        out[c] = front + clear * back
    product = clear_mine * clear_other
    out[3] = 1.0 - product if last else product


def blend(flags, mine, other, bit, last):
    return pl.pallas_call(
        functools.partial(blend_kernel, bit, last),
        out_shape=jax.ShapeDtypeStruct(mine.shape, jnp.float32),
        in_specs=[VMEM] * 3,
        out_specs=VMEM,
        compiler_params=pltpu.CompilerParams(vmem_limit_bytes=VMEM_LIMIT),
        name="blend",
    )(flags, mine, other)


def shards(density, material, color_table, extinction_table, order):
    planes, rows, cols = density.shape
    counts = {axis: lax.axis_size(axis) for axis in ("bx", "by", "bz")}
    slabs = counts["bz"]
    padded, y_own, xa, xb, za, zb, tables, flags = faces(
        order, density, color_table, extinction_table, counts
    )
    pairs = {axis: swaps(counts[axis]) for axis in counts}
    xa = lax.ppermute(xa, "bx", pairs["bx"][0])
    xb = lax.ppermute(xb, "bx", pairs["bx"][1])
    za = lax.ppermute(za, "bz", pairs["bz"][0])
    if slabs > 2:
        zb = lax.ppermute(zb, "bz", pairs["bz"][1])
    ya = lax.ppermute(y_own, "by", pairs["by"][0])
    yb = lax.ppermute(y_own, "by", pairs["by"][1])
    lit, slope_y, through = local(padded, material, tables, flags, planes * slabs)
    halos = (xa, xb, za, zb, ya, yb)
    padded, edge, give = shade_give(padded, halos, lit, slope_y, through)
    keep = shade_keep(padded, edge, lit, slope_y, through)
    block_rows = rows // slabs
    levels = slabs.bit_length() - 1
    my_slab = lax.axis_index("bz")
    for bit in range(levels):
        flip = [(i, i ^ (1 << bit)) for i in range(slabs)]
        received = lax.ppermute(give, "bz", flip)
        holding = blend(flags, keep, received, bit, bit == levels - 1)
        if bit < levels - 1:
            paired = holding.reshape(4, -1, 2, block_rows, cols)
            half = jnp.bitwise_and(jnp.right_shift(my_slab, bit + 1), 1)
            take = lambda which: lax.dynamic_index_in_dim(paired, which, 2, keepdims=False)
            keep, give = (take(which).reshape(4, -1, cols) for which in (half, 1 - half))
    return holding


def solution(mesh):
    placed = (P("bz", "bx", "by"), P("bz", "bx", "by"), P(), P(), P("bx", "by", None))
    return jax.shard_map(
        shards, mesh=mesh, in_specs=placed, out_specs=P(None, ("bx", "bz"), "by"), check_vma=False
    )
```

```python
import functools
import math

import jax
import jax.numpy as jnp
from jax import lax
from jax.experimental import pallas as pl
from jax.experimental.pallas import tpu as pltpu
from jax.sharding import PartitionSpec as P

LANES = 128
SUBLANES = 8
PAD = 8
REACH = 2
COLOR_UNIT = 4096.0
EXTINCTION_UNIT = 2048.0
VMEM_LIMIT = 12 * 2**20

VMEM = pl.BlockSpec(memory_space=pltpu.VMEM)
HBM = pl.BlockSpec(memory_space=pltpu.HBM)


def lane_index():
    return lax.broadcasted_iota(jnp.int32, (SUBLANES, LANES), 1)


def is_odd(axis):
    return jnp.bitwise_and(lax.axis_index(axis), 1) == 1


def swaps(count):
    first = [(i, i ^ 1) for i in range(count)]
    second = [(i, i + 1 if i % 2 else i - 1) for i in range(1, count - 1)]
    return first, second


def faces_kernel(counts, order, density, colors, extinction, padded, y_out, xa, xb, za, zb, tables, flags, place, hues, thick, arrived):
    planes, rows, _ = density.shape
    parts = arrived.shape[0] - 3
    step = rows // parts
    copies = [
        pltpu.make_async_copy(
            density.at[:, pl.ds(k * step, step), :],
            padded.at[pl.ds(REACH, planes), pl.ds(PAD + k * step, step), :],
            arrived.at[k],
        )
        for k in range(parts)
    ]
    small = [
        pltpu.make_async_copy(source, target, arrived.at[parts + k])
        for k, (source, target) in enumerate(((order, place), (colors, hues), (extinction, thick)))
    ]
    for copy in copies + small:
        copy.start()
    slot = jnp.right_shift(lane_index(), 2)
    for k in range(parts):
        copies[k].wait()
        for tile in range(step // SUBLANES):
            row = k * step + tile * SUBLANES
            packed = jnp.zeros((SUBLANES, LANES), jnp.float32)
            for z in range(planes):
                plane = padded[REACH + z, PAD + row : PAD + row + SUBLANES, :]
                packed = jnp.where(slot == z, pltpu.roll(plane, (4 * z + REACH) % LANES, 1), packed)
            y_out[row : row + SUBLANES, :] = packed
    odd_x, odd_z = is_odd("bx"), is_odd("bz")
    low_x, high_x = PAD, PAD + rows - REACH
    low_z, high_z = REACH, planes
    for out, start in ((xa, jnp.where(odd_x, low_x, high_x)), (xb, jnp.where(odd_x, high_x, low_x))):
        for z in range(planes):
            out[REACH * z : REACH * (z + 1), :] = padded[REACH + z, pl.ds(start, REACH), :]
    for out, start in ((za, jnp.where(odd_z, low_z, high_z)), (zb, jnp.where(odd_z, high_z, low_z))):
        if out is zb and counts["bz"] == 2:
            continue
        for layer in range(REACH):
            out[layer] = padded[start + layer, PAD : PAD + rows, :]
    if counts["bz"] == 2:
        zb[...] = jnp.zeros(zb.shape, jnp.float32)
    for copy in small:
        copy.wait()
    slabs = counts["bz"]
    backward = (place[0, 0, 0] > place[0, 0, slabs - 1]).astype(jnp.float32)
    rank = jnp.bitwise_xor(lax.axis_index("bz"), place[0, 0, 0])
    flags[0] = jnp.full((SUBLANES, LANES), backward, jnp.float32)
    for bit in range(slabs.bit_length() - 1):
        behind = jnp.bitwise_and(jnp.right_shift(rank, bit), 1).astype(jnp.float32)
        flags[1 + bit] = jnp.full((SUBLANES, LANES), behind, jnp.float32)
    color = (hues[...].astype(jnp.float32) * COLOR_UNIT).astype(jnp.int32)
    dense = (thick[...].astype(jnp.float32) * EXTINCTION_UNIT).astype(jnp.int32)
    for k, table in enumerate((color[0:1] * 65536 + color[1:2], color[2:3] * 65536 + dense)):
        for part in range(2):
            tables[2 * k + part] = jnp.broadcast_to(
                table[:, part * LANES : (part + 1) * LANES], (SUBLANES, LANES)
            )


def faces(order, density, colors, extinction, counts):
    planes, rows, cols = density.shape
    shape = lambda *dims: pltpu.VMEM(dims, jnp.float32)
    z_rows = rows if counts["bz"] > 2 else SUBLANES
    return pl.pallas_call(
        functools.partial(faces_kernel, counts),
        out_shape=(
            shape(planes + 2 * REACH, rows + 2 * PAD, cols),
            shape(rows, LANES),
            shape(REACH * planes, cols),
            shape(REACH * planes, cols),
            shape(REACH, rows, cols),
            shape(REACH, z_rows, cols),
            pltpu.VMEM((4, SUBLANES, LANES), jnp.int32),
            shape(counts["bz"].bit_length(), SUBLANES, LANES),
        ),
        in_specs=[HBM] * 4,
        out_specs=(VMEM,) * 8,
        scratch_shapes=[
            pltpu.SMEM(order.shape, jnp.int32),
            pltpu.VMEM(colors.shape, colors.dtype),
            pltpu.VMEM(extinction.shape, extinction.dtype),
            pltpu.SemaphoreType.DMA((7,)),
        ],
        compiler_params=pltpu.CompilerParams(vmem_limit_bytes=VMEM_LIMIT),
        name="faces",
    )(*(pltpu.with_memory_space_constraint(a, pltpu.HBM) for a in (order, density, colors, extinction)))


def local_kernel(total_planes, padded, material, tables, flags, lit, slope_y, through):
    planes, rows, _ = material.shape
    backward = jnp.max(flags[0]) > 0.5
    k = jnp.bitwise_and(lax.broadcasted_iota(jnp.int32, (2 * LANES, LANES), 0), LANES - 1)
    gap = k - lax.broadcasted_iota(jnp.int32, (2 * LANES, LANES), 1)
    band = jnp.where(gap == 1, 8.0, jnp.where(gap == -1, -8.0, 0.0))
    band = band + jnp.where(gap == 2, -1.0, jnp.where(gap == -2, 1.0, 0.0))
    band = band.astype(jnp.bfloat16)
    scale = -3.0 * math.log2(math.e) / (EXTINCTION_UNIT * total_planes)

    def take(first, low, upper):
        found = [
            jnp.take_along_axis(tables[first + k], low, axis=1, mode="promise_in_bounds")
            for k in range(2)
        ]
        return jnp.where(upper, found[1], found[0])

    def tile(index, carry):
        top = pl.multiple_of(index * 2 * SUBLANES, 2 * SUBLANES)
        coarse, fine = [], []
        for z in range(planes):
            plane = padded[REACH + z, pl.ds(PAD + top, 2 * SUBLANES), :]
            rounded = plane.astype(jnp.bfloat16)
            coarse.append(rounded)
            fine.append((plane - rounded.astype(jnp.float32)).astype(jnp.bfloat16))
        both = jnp.concatenate(
            [jnp.concatenate(coarse, axis=0), jnp.concatenate(fine, axis=0)], axis=1
        )
        slopes = jnp.dot(both, band, preferred_element_type=jnp.float32)
        for z in range(planes):
            slope_y[z, pl.ds(top, 2 * SUBLANES), :] = slopes[2 * SUBLANES * z : 2 * SUBLANES * (z + 1)]
        for part in range(2):
            row = pl.multiple_of(top + part * SUBLANES, SUBLANES)
            clear = jnp.ones((SUBLANES, LANES), jnp.float32)
            for visit in range(planes):
                z = jnp.where(backward, planes - 1 - visit, visit)
                density = padded[REACH + z, pl.ds(PAD + row, SUBLANES), :]
                label = material[z, pl.ds(row, SUBLANES), :]
                low = jnp.bitwise_and(label, LANES - 1)
                upper = label >= LANES
                rg = take(0, low, upper)
                be = take(2, low, upper)
                extinct = jnp.bitwise_and(be, 65535).astype(jnp.float32)
                after = clear * jnp.exp2(extinct * (density * scale))
                stopped = clear - after
                here = (z, pl.ds(row, SUBLANES), slice(None))
                lit[(0, *here)] = stopped * jnp.right_shift(rg, 16).astype(jnp.float32)
                lit[(1, *here)] = stopped * jnp.bitwise_and(rg, 65535).astype(jnp.float32)
                lit[(2, *here)] = stopped * jnp.right_shift(be, 16).astype(jnp.float32)
                clear = after
            through[pl.ds(row, SUBLANES), :] = clear
        return carry

    lax.fori_loop(0, rows // SUBLANES // 2, tile, 0)


def local(padded, material, tables, flags, total_planes):
    planes, rows, cols = material.shape
    shape = lambda *dims: jax.ShapeDtypeStruct(dims, jnp.float32)
    return pl.pallas_call(
        functools.partial(local_kernel, total_planes),
        out_shape=(shape(3, planes, rows, cols), shape(planes, rows, cols), shape(rows, cols)),
        in_specs=[VMEM] * 4,
        out_specs=(VMEM,) * 3,
        compiler_params=pltpu.CompilerParams(vmem_limit_bytes=VMEM_LIMIT),
        cost_estimate=pl.CostEstimate(
            flops=20 * planes * rows * cols,
            bytes_accessed=2**22,
            transcendentals=planes * rows * cols,
        ),
        name="local",
    )(padded, material, tables, flags)


def put_halo(padded, xa, xb, za, zb, ya, yb, edge, planes, rows):
    odd_x, odd_y, odd_z = is_odd("bx"), is_odd("by"), is_odd("bz")
    for z in range(planes):
        first, second = xa[REACH * z : REACH * (z + 1), :], xb[REACH * z : REACH * (z + 1), :]
        padded[REACH + z, PAD - REACH : PAD, :] = jnp.where(odd_x, first, second)
        padded[REACH + z, PAD + rows : PAD + rows + REACH, :] = jnp.where(odd_x, second, first)
    for layer in range(REACH):
        first = za[layer]
        second = zb[layer] if zb.shape == za.shape else jnp.zeros_like(first)
        padded[layer, PAD : PAD + rows, :] = jnp.where(odd_z, first, second)
        padded[REACH + planes + layer, PAD : PAD + rows, :] = jnp.where(odd_z, second, first)
    side = jnp.bitwise_and(lane_index(), 3)
    for row in range(0, rows, SUBLANES):
        first, second = ya[row : row + SUBLANES, :], yb[row : row + SUBLANES, :]
        near = jnp.where((side < 2) == odd_y, first, second)
        ahead1, ahead2 = pltpu.roll(near, LANES - 1, 1), pltpu.roll(near, LANES - 2, 1)
        behind1, behind2 = pltpu.roll(near, 1, 1), pltpu.roll(near, 2, 1)
        edge[row : row + SUBLANES, :] = jnp.where(
            side == 0,
            -ahead2,
            jnp.where(
                side == 1,
                8.0 * ahead1 - ahead2,
                jnp.where(side == 2, behind2 - 8.0 * behind1, behind2),
            ),
        )


def shade_half(padded, edge, lit, slope_y, through, out, giving):
    _, planes, rows, _ = lit.shape
    block_rows = rows // lax.axis_size("bz")
    half = jnp.bitwise_and(lax.axis_index("bz") + (1 if giving else 0), 1)
    lane = lane_index()
    at_edge = jnp.logical_or(lane < REACH, lane >= LANES - REACH)

    def pair(index, carry):
        for part in range(2):
            to = pl.multiple_of((2 * index + part) * SUBLANES, SUBLANES)
            group = lax.div(to, block_rows)
            row = pl.multiple_of((group + half) * block_rows + to, SUBLANES)
            beside = edge[pl.ds(row, SUBLANES), :]
            sums = [jnp.zeros((SUBLANES, LANES), jnp.float32) for _ in range(3)]
            for z in range(planes):
                at = lambda dz, dx: padded[REACH + z + dz, pl.ds(PAD + row + dx, SUBLANES), :]
                sz = 8.0 * (at(1, 0) - at(-1, 0)) - (at(2, 0) - at(-2, 0))
                sx = 8.0 * (at(0, 1) - at(0, -1)) - (at(0, 2) - at(0, -2))
                outer = pltpu.roll(beside, (-4 * z - REACH) % LANES, 1)
                sy = slope_y[z, pl.ds(row, SUBLANES), :] + jnp.where(at_edge, outer, 0.0)
                size = sx * sx + sy * sy + sz * sz
                facing = jnp.abs(0.432 * sx + 0.54 * sy + 0.576 * sz)
                shading = 0.1 + facing * lax.rsqrt(jnp.maximum(size, 36.0))
                for c in range(3):
                    sums[c] = sums[c] + shading * lit[c, z, pl.ds(row, SUBLANES), :]
            for c in range(3):
                out[c, pl.ds(to, SUBLANES), :] = sums[c] * (1.0 / COLOR_UNIT)
            out[3, pl.ds(to, SUBLANES), :] = through[pl.ds(row, SUBLANES), :]
        return carry

    lax.fori_loop(0, rows // 4 // SUBLANES, pair, 0)


def shade_give_kernel(padded_in, xa, xb, za, zb, ya, yb, lit, slope_y, through, padded, edge, give):
    _, planes, rows, _ = lit.shape
    del padded_in
    put_halo(padded, xa, xb, za, zb, ya, yb, edge, planes, rows)
    shade_half(padded, edge, lit, slope_y, through, give, True)


def shade_keep_kernel(padded, edge, lit, slope_y, through, keep):
    shade_half(padded, edge, lit, slope_y, through, keep, False)


def shade_give(padded, halos, lit, slope_y, through):
    _, _, rows, cols = lit.shape
    shape = lambda *dims: jax.ShapeDtypeStruct(dims, jnp.float32)
    return pl.pallas_call(
        shade_give_kernel,
        out_shape=(shape(*padded.shape), shape(rows, LANES), shape(4, rows // 2, cols)),
        in_specs=[VMEM] * 10,
        out_specs=(VMEM,) * 3,
        input_output_aliases={0: 0},
        compiler_params=pltpu.CompilerParams(vmem_limit_bytes=VMEM_LIMIT),
        name="shade_give",
    )(padded, *halos, lit, slope_y, through)


def shade_keep(padded, edge, lit, slope_y, through):
    _, planes, rows, cols = lit.shape
    return pl.pallas_call(
        shade_keep_kernel,
        out_shape=jax.ShapeDtypeStruct((4, rows // 2, cols), jnp.float32),
        in_specs=[VMEM] * 5,
        out_specs=VMEM,
        compiler_params=pltpu.CompilerParams(vmem_limit_bytes=VMEM_LIMIT),
        cost_estimate=pl.CostEstimate(
            flops=20 * planes * rows * cols, bytes_accessed=2**22, transcendentals=0
        ),
        name="shade_keep",
    )(padded, edge, lit, slope_y, through)


def blend_kernel(bit, last, flags, mine, other, out):
    clear_mine, clear_other = mine[3], other[3]
    behind = jnp.broadcast_to(flags[1 + bit, 0:1, :], clear_mine.shape) > 0.5
    clear = jnp.where(behind, clear_other, clear_mine)
    for c in range(3):
        front = jnp.where(behind, other[c], mine[c])
        back = jnp.where(behind, mine[c], other[c])
        out[c] = front + clear * back
    product = clear_mine * clear_other
    out[3] = 1.0 - product if last else product


def blend(flags, mine, other, bit, last):
    return pl.pallas_call(
        functools.partial(blend_kernel, bit, last),
        out_shape=jax.ShapeDtypeStruct(mine.shape, jnp.float32),
        in_specs=[VMEM] * 3,
        out_specs=VMEM,
        compiler_params=pltpu.CompilerParams(vmem_limit_bytes=VMEM_LIMIT),
        name="blend",
    )(flags, mine, other)


def shards(density, material, color_table, extinction_table, order):
    planes, rows, cols = density.shape
    counts = {axis: lax.axis_size(axis) for axis in ("bx", "by", "bz")}
    slabs = counts["bz"]
    padded, y_own, xa, xb, za, zb, tables, flags = faces(
        order, density, color_table, extinction_table, counts
    )
    pairs = {axis: swaps(counts[axis]) for axis in counts}
    xa = lax.ppermute(xa, "bx", pairs["bx"][0])
    xb = lax.ppermute(xb, "bx", pairs["bx"][1])
    za = lax.ppermute(za, "bz", pairs["bz"][0])
    if slabs > 2:
        zb = lax.ppermute(zb, "bz", pairs["bz"][1])
    ya = lax.ppermute(y_own, "by", pairs["by"][0])
    yb = lax.ppermute(y_own, "by", pairs["by"][1])
    lit, slope_y, through = local(padded, material, tables, flags, planes * slabs)
    halos = (xa, xb, za, zb, ya, yb)
    padded, edge, give = shade_give(padded, halos, lit, slope_y, through)
    keep = shade_keep(padded, edge, lit, slope_y, through)
    block_rows = rows // slabs
    levels = slabs.bit_length() - 1
    my_slab = lax.axis_index("bz")
    for bit in range(levels):
        flip = [(i, i ^ (1 << bit)) for i in range(slabs)]
        received = lax.ppermute(give, "bz", flip)
        holding = blend(flags, keep, received, bit, bit == levels - 1)
        if bit < levels - 1:
            paired = holding.reshape(4, -1, 2, block_rows, cols)
            half = jnp.bitwise_and(jnp.right_shift(my_slab, bit + 1), 1)
            take = lambda which: lax.dynamic_index_in_dim(paired, which, 2, keepdims=False)
            keep, give = (take(which).reshape(4, -1, cols) for which in (half, 1 - half))
    return holding


def solution(mesh):
    placed = (P("bz", "bx", "by"), P("bz", "bx", "by"), P(), P(), P("bx", "by", None))
    return jax.shard_map(
        shards, mesh=mesh, in_specs=placed, out_specs=P(None, ("bx", "bz"), "by"), check_vma=False
    )
```

```python
import functools
import math

import jax
import jax.numpy as jnp
from jax import lax
from jax.experimental import pallas as pl
from jax.experimental.pallas import tpu as pltpu
from jax.sharding import PartitionSpec as P

LANES = 128
SUBLANES = 8
TILE = 16
PAD = 8
REACH = 2
COLOR_UNIT = 4096.0
EXTINCTION_UNIT = 2048.0
VMEM_LIMIT = 12 * 2**20

VMEM = pl.BlockSpec(memory_space=pltpu.VMEM)
HBM = pl.BlockSpec(memory_space=pltpu.HBM)


def lane_index():
    return lax.broadcasted_iota(jnp.int32, (SUBLANES, LANES), 1)


def is_odd(axis):
    return jnp.bitwise_and(lax.axis_index(axis), 1) == 1


def swaps(count):
    first = [(i, i ^ 1) for i in range(count)]
    second = [(i, i + 1 if i % 2 else i - 1) for i in range(1, count - 1)]
    return first, second


def faces_kernel(counts, order, density, colors, extinction, padded, y_out, xa, xb, za, zb, tables, flags, place, hues, thick, arrived):
    planes, rows, _ = density.shape
    parts = arrived.shape[0] - 3
    step = rows // parts
    copies = [
        pltpu.make_async_copy(
            density.at[:, pl.ds(k * step, step), :],
            padded.at[pl.ds(REACH, planes), pl.ds(PAD + k * step, step), :],
            arrived.at[k],
        )
        for k in range(parts)
    ]
    small = [
        pltpu.make_async_copy(source, target, arrived.at[parts + k])
        for k, (source, target) in enumerate(((order, place), (colors, hues), (extinction, thick)))
    ]
    for copy in copies + small:
        copy.start()
    slot = jnp.right_shift(lane_index(), 2)
    for k in range(parts):
        copies[k].wait()
        for tile in range(step // SUBLANES):
            row = k * step + tile * SUBLANES
            packed = jnp.zeros((SUBLANES, LANES), jnp.float32)
            for z in range(planes):
                plane = padded[REACH + z, PAD + row : PAD + row + SUBLANES, :]
                packed = jnp.where(slot == z, pltpu.roll(plane, (4 * z + REACH) % LANES, 1), packed)
            y_out[row : row + SUBLANES, :] = packed
    odd_x, odd_z = is_odd("bx"), is_odd("bz")
    low_x, high_x = PAD, PAD + rows - REACH
    low_z, high_z = REACH, planes
    for out, start in ((xa, jnp.where(odd_x, low_x, high_x)), (xb, jnp.where(odd_x, high_x, low_x))):
        for z in range(planes):
            out[REACH * z : REACH * (z + 1), :] = padded[REACH + z, pl.ds(start, REACH), :]
    for out, start in ((za, jnp.where(odd_z, low_z, high_z)), (zb, jnp.where(odd_z, high_z, low_z))):
        if out is zb and counts["bz"] == 2:
            continue
        for layer in range(REACH):
            out[layer] = padded[start + layer, PAD : PAD + rows, :]
    if counts["bz"] == 2:
        zb[...] = jnp.zeros(zb.shape, jnp.float32)
    for copy in small:
        copy.wait()
    slabs = counts["bz"]
    backward = (place[0, 0, 0] > place[0, 0, slabs - 1]).astype(jnp.float32)
    rank = jnp.bitwise_xor(lax.axis_index("bz"), place[0, 0, 0])
    flags[0] = jnp.full((SUBLANES, LANES), backward, jnp.float32)
    for bit in range(slabs.bit_length() - 1):
        behind = jnp.bitwise_and(jnp.right_shift(rank, bit), 1).astype(jnp.float32)
        flags[1 + bit] = jnp.full((SUBLANES, LANES), behind, jnp.float32)
    color = (hues[...].astype(jnp.float32) * COLOR_UNIT).astype(jnp.int32)
    dense = (thick[...].astype(jnp.float32) * EXTINCTION_UNIT).astype(jnp.int32)
    for k, table in enumerate((color[0:1] * 65536 + color[1:2], color[2:3] * 65536 + dense)):
        for part in range(2):
            tables[2 * k + part] = jnp.broadcast_to(
                table[:, part * LANES : (part + 1) * LANES], (SUBLANES, LANES)
            )


def faces(order, density, colors, extinction, counts):
    planes, rows, cols = density.shape
    shape = lambda *dims: pltpu.VMEM(dims, jnp.float32)
    z_rows = rows if counts["bz"] > 2 else SUBLANES
    return pl.pallas_call(
        functools.partial(faces_kernel, counts),
        out_shape=(
            shape(planes + 2 * REACH, rows + 2 * PAD, cols),
            shape(rows, LANES),
            shape(REACH * planes, cols),
            shape(REACH * planes, cols),
            shape(REACH, rows, cols),
            shape(REACH, z_rows, cols),
            pltpu.VMEM((4, SUBLANES, LANES), jnp.int32),
            shape(counts["bz"].bit_length(), SUBLANES, LANES),
        ),
        in_specs=[HBM] * 4,
        out_specs=(VMEM,) * 8,
        scratch_shapes=[
            pltpu.SMEM(order.shape, jnp.int32),
            pltpu.VMEM(colors.shape, colors.dtype),
            pltpu.VMEM(extinction.shape, extinction.dtype),
            pltpu.SemaphoreType.DMA((7,)),
        ],
        compiler_params=pltpu.CompilerParams(vmem_limit_bytes=VMEM_LIMIT),
        name="faces",
    )(*(pltpu.with_memory_space_constraint(a, pltpu.HBM) for a in (order, density, colors, extinction)))


def half_rows(tile_rows, index, rows, giving):
    block_rows = rows // lax.axis_size("bz")
    half = jnp.bitwise_and(lax.axis_index("bz") + (1 if giving else 0), 1)
    to = pl.multiple_of(index * tile_rows, tile_rows)
    row = (lax.div(to, block_rows) + half) * block_rows + to
    return to, pl.multiple_of(row, tile_rows)


def band_matrix():
    k = jnp.bitwise_and(lax.broadcasted_iota(jnp.int32, (2 * LANES, LANES), 0), LANES - 1)
    gap = k - lax.broadcasted_iota(jnp.int32, (2 * LANES, LANES), 1)
    band = jnp.where(gap == 1, 8.0, jnp.where(gap == -1, -8.0, 0.0))
    band = band + jnp.where(gap == 2, -1.0, jnp.where(gap == -2, 1.0, 0.0))
    return band.astype(jnp.bfloat16)


def slopes_along_y(padded, band, row, planes):
    coarse, fine = [], []
    for z in range(planes):
        plane = padded[REACH + z, pl.ds(PAD + row, TILE), :]
        rounded = plane.astype(jnp.bfloat16)
        coarse.append(rounded)
        fine.append((plane - rounded.astype(jnp.float32)).astype(jnp.bfloat16))
    both = jnp.concatenate([jnp.concatenate(coarse, axis=0), jnp.concatenate(fine, axis=0)], axis=1)
    return jnp.dot(both, band, preferred_element_type=jnp.float32)


def take(tables, first, low, upper):
    found = [
        jnp.take_along_axis(tables[first + k], low, axis=1, mode="promise_in_bounds")
        for k in range(2)
    ]
    return jnp.where(upper, found[1], found[0])


def absorb(padded, material, tables, z, row, clear, scale):
    density = padded[REACH + z, pl.ds(PAD + row, SUBLANES), :]
    label = material[z, pl.ds(row, SUBLANES), :]
    low = jnp.bitwise_and(label, LANES - 1)
    upper = label >= LANES
    rg = take(tables, 0, low, upper)
    be = take(tables, 2, low, upper)
    extinct = jnp.bitwise_and(be, 65535).astype(jnp.float32)
    after = clear * jnp.exp2(extinct * (density * scale))
    stopped = clear - after
    whole = (jnp.right_shift(rg, 16), jnp.bitwise_and(rg, 65535), jnp.right_shift(be, 16))
    return [stopped * part.astype(jnp.float32) for part in whole], after


def shading_at(padded, slope_y, beside, at_edge, z, row):
    at = lambda dz, dx: padded[REACH + z + dz, pl.ds(PAD + row + dx, SUBLANES), :]
    sz = 8.0 * (at(1, 0) - at(-1, 0)) - (at(2, 0) - at(-2, 0))
    sx = 8.0 * (at(0, 1) - at(0, -1)) - (at(0, 2) - at(0, -2))
    outer = pltpu.roll(beside, jnp.bitwise_and(-4 * z - REACH, LANES - 1), 1)
    sy = slope_y + jnp.where(at_edge, outer, 0.0)
    size = sx * sx + sy * sy + sz * sz
    facing = jnp.abs(0.432 * sx + 0.54 * sy + 0.576 * sz)
    return 0.1 + facing * lax.rsqrt(jnp.maximum(size, 36.0))


def edge_lanes():
    lane = lane_index()
    return jnp.logical_or(lane < REACH, lane >= LANES - REACH)


def scale_of(total_planes):
    return -3.0 * math.log2(math.e) / (EXTINCTION_UNIT * total_planes)


def local_give_kernel(total_planes, padded, material, tables, flags, lit, slope_y, through):
    planes, rows, _ = material.shape
    backward = jnp.max(flags[0]) > 0.5
    band = band_matrix()
    scale = scale_of(total_planes)

    def tile(index, carry):
        to, row = half_rows(TILE, index, rows, True)
        slopes = slopes_along_y(padded, band, row, planes)
        for z in range(planes):
            slope_y[z, pl.ds(to, TILE), :] = slopes[TILE * z : TILE * (z + 1)]
        for part in range(0, TILE, SUBLANES):
            clear = jnp.ones((SUBLANES, LANES), jnp.float32)
            for visit in range(planes):
                z = jnp.where(backward, planes - 1 - visit, visit)
                light, clear = absorb(padded, material, tables, z, row + part, clear, scale)
                for c in range(3):
                    lit[c, z, pl.ds(to + part, SUBLANES), :] = light[c]
            through[pl.ds(to + part, SUBLANES), :] = clear
        return carry

    lax.fori_loop(0, rows // 2 // TILE, tile, 0)


def local_give(padded, material, tables, flags, total_planes):
    planes, rows, cols = material.shape
    shape = lambda *dims: pltpu.VMEM(dims, jnp.float32)
    return pl.pallas_call(
        functools.partial(local_give_kernel, total_planes),
        out_shape=(
            shape(3, planes, rows // 2, cols),
            shape(planes, rows // 2, cols),
            shape(rows // 2, cols),
        ),
        in_specs=[VMEM] * 4,
        out_specs=(VMEM,) * 3,
        compiler_params=pltpu.CompilerParams(vmem_limit_bytes=VMEM_LIMIT),
        cost_estimate=pl.CostEstimate(
            flops=20 * planes * rows * cols,
            bytes_accessed=2**22,
            transcendentals=planes * rows * cols,
        ),
        name="local_give",
    )(padded, material, tables, flags)


def put_halo(padded, xa, xb, za, zb, ya, yb, edge, planes, rows):
    odd_x, odd_y, odd_z = is_odd("bx"), is_odd("by"), is_odd("bz")
    for z in range(planes):
        first, second = xa[REACH * z : REACH * (z + 1), :], xb[REACH * z : REACH * (z + 1), :]
        padded[REACH + z, PAD - REACH : PAD, :] = jnp.where(odd_x, first, second)
        padded[REACH + z, PAD + rows : PAD + rows + REACH, :] = jnp.where(odd_x, second, first)
    for layer in range(REACH):
        first = za[layer]
        second = zb[layer] if zb.shape == za.shape else jnp.zeros_like(first)
        padded[layer, PAD : PAD + rows, :] = jnp.where(odd_z, first, second)
        padded[REACH + planes + layer, PAD : PAD + rows, :] = jnp.where(odd_z, second, first)
    side = jnp.bitwise_and(lane_index(), 3)
    for row in range(0, rows, SUBLANES):
        first, second = ya[row : row + SUBLANES, :], yb[row : row + SUBLANES, :]
        near = jnp.where((side < 2) == odd_y, first, second)
        ahead1, ahead2 = pltpu.roll(near, LANES - 1, 1), pltpu.roll(near, LANES - 2, 1)
        behind1, behind2 = pltpu.roll(near, 1, 1), pltpu.roll(near, 2, 1)
        edge[row : row + SUBLANES, :] = jnp.where(
            side == 0,
            -ahead2,
            jnp.where(
                side == 1,
                8.0 * ahead1 - ahead2,
                jnp.where(side == 2, behind2 - 8.0 * behind1, behind2),
            ),
        )


def shade_give_kernel(padded_in, xa, xb, za, zb, ya, yb, lit, slope_y, through, padded, edge, give):
    _, planes, half, _ = lit.shape
    rows = 2 * half
    del padded_in
    put_halo(padded, xa, xb, za, zb, ya, yb, edge, planes, rows)
    at_edge = edge_lanes()

    def tile(index, carry):
        to, row = half_rows(TILE, index, rows, True)
        for part in range(0, TILE, SUBLANES):
            beside = edge[pl.ds(row + part, SUBLANES), :]
            place = pl.ds(to + part, SUBLANES)
            sums = [jnp.zeros((SUBLANES, LANES), jnp.float32) for _ in range(3)]
            for z in range(planes):
                shading = shading_at(padded, slope_y[z, place, :], beside, at_edge, z, row + part)
                for c in range(3):
                    sums[c] = sums[c] + shading * lit[c, z, place, :]
            for c in range(3):
                give[c, place, :] = sums[c] * (1.0 / COLOR_UNIT)
            give[3, place, :] = through[place, :]
        return carry

    lax.fori_loop(0, half // TILE, tile, 0)


def shade_give(padded, halos, lit, slope_y, through):
    _, _, half, cols = lit.shape
    shape = lambda *dims: pltpu.VMEM(dims, jnp.float32)
    return pl.pallas_call(
        shade_give_kernel,
        out_shape=(shape(*padded.shape), shape(2 * half, LANES), shape(4, half, cols)),
        in_specs=[VMEM] * 10,
        out_specs=(VMEM,) * 3,
        input_output_aliases={0: 0},
        compiler_params=pltpu.CompilerParams(vmem_limit_bytes=VMEM_LIMIT),
        name="shade_give",
    )(padded, *halos, lit, slope_y, through)


def keep_kernel(total_planes, padded, edge, material, tables, flags, keep, slope_y):
    planes, rows, _ = material.shape
    backward = jnp.max(flags[0]) > 0.5
    band = band_matrix()
    scale = scale_of(total_planes)
    at_edge = edge_lanes()

    def tile(index, carry):
        to, row = half_rows(TILE, index, rows, False)
        slope_y[...] = slopes_along_y(padded, band, row, planes).reshape(planes, TILE, LANES)
        for part in range(0, TILE, SUBLANES):
            beside = edge[pl.ds(row + part, SUBLANES), :]
            place = pl.ds(to + part, SUBLANES)
            clear = jnp.ones((SUBLANES, LANES), jnp.float32)
            sums = [jnp.zeros((SUBLANES, LANES), jnp.float32) for _ in range(3)]
            for visit in range(planes):
                z = jnp.where(backward, planes - 1 - visit, visit)
                slope = slope_y[z, part : part + SUBLANES, :]
                light, clear = absorb(padded, material, tables, z, row + part, clear, scale)
                shading = shading_at(padded, slope, beside, at_edge, z, row + part)
                for c in range(3):
                    sums[c] = sums[c] + shading * light[c]
            for c in range(3):
                keep[c, place, :] = sums[c] * (1.0 / COLOR_UNIT)
            keep[3, place, :] = clear
        return carry

    lax.fori_loop(0, rows // 2 // TILE, tile, 0)


def shade_keep(padded, edge, material, tables, flags, total_planes):
    planes, rows, cols = material.shape
    return pl.pallas_call(
        functools.partial(keep_kernel, total_planes),
        out_shape=pltpu.VMEM((4, rows // 2, cols), jnp.float32),
        in_specs=[VMEM] * 5,
        out_specs=VMEM,
        scratch_shapes=[pltpu.VMEM((planes, TILE, LANES), jnp.float32)],
        compiler_params=pltpu.CompilerParams(vmem_limit_bytes=VMEM_LIMIT),
        cost_estimate=pl.CostEstimate(
            flops=40 * planes * rows * cols,
            bytes_accessed=2**22,
            transcendentals=planes * rows * cols,
        ),
        name="keep",
    )(padded, edge, material, tables, flags)


def blend_kernel(bit, last, flags, mine, other, out):
    clear_mine, clear_other = mine[3], other[3]
    behind = jnp.broadcast_to(flags[1 + bit, 0:1, :], clear_mine.shape) > 0.5
    clear = jnp.where(behind, clear_other, clear_mine)
    for c in range(3):
        front = jnp.where(behind, other[c], mine[c])
        back = jnp.where(behind, mine[c], other[c])
        out[c] = front + clear * back
    product = clear_mine * clear_other
    out[3] = 1.0 - product if last else product


def blend(flags, mine, other, bit, last):
    return pl.pallas_call(
        functools.partial(blend_kernel, bit, last),
        out_shape=jax.ShapeDtypeStruct(mine.shape, jnp.float32),
        in_specs=[VMEM] * 3,
        out_specs=VMEM,
        compiler_params=pltpu.CompilerParams(vmem_limit_bytes=VMEM_LIMIT),
        name="blend",
    )(flags, mine, other)


def shards(density, material, color_table, extinction_table, order):
    planes, rows, cols = density.shape
    counts = {axis: lax.axis_size(axis) for axis in ("bx", "by", "bz")}
    slabs = counts["bz"]
    padded, y_own, xa, xb, za, zb, tables, flags = faces(
        order, density, color_table, extinction_table, counts
    )
    pairs = {axis: swaps(counts[axis]) for axis in counts}
    xa = lax.ppermute(xa, "bx", pairs["bx"][0])
    xb = lax.ppermute(xb, "bx", pairs["bx"][1])
    za = lax.ppermute(za, "bz", pairs["bz"][0])
    if slabs > 2:
        zb = lax.ppermute(zb, "bz", pairs["bz"][1])
    ya = lax.ppermute(y_own, "by", pairs["by"][0])
    yb = lax.ppermute(y_own, "by", pairs["by"][1])
    lit, slope_y, through = local_give(padded, material, tables, flags, planes * slabs)
    halos = (xa, xb, za, zb, ya, yb)
    padded, edge, give = shade_give(padded, halos, lit, slope_y, through)
    keep = shade_keep(padded, edge, material, tables, flags, planes * slabs)
    block_rows = rows // slabs
    levels = slabs.bit_length() - 1
    my_slab = lax.axis_index("bz")
    for bit in range(levels):
        flip = [(i, i ^ (1 << bit)) for i in range(slabs)]
        received = lax.ppermute(give, "bz", flip)
        holding = blend(flags, keep, received, bit, bit == levels - 1)
        if bit < levels - 1:
            paired = holding.reshape(4, -1, 2, block_rows, cols)
            half = jnp.bitwise_and(jnp.right_shift(my_slab, bit + 1), 1)
            take = lambda which: lax.dynamic_index_in_dim(paired, which, 2, keepdims=False)
            keep, give = (take(which).reshape(4, -1, cols) for which in (half, 1 - half))
    return holding


def solution(mesh):
    placed = (P("bz", "bx", "by"), P("bz", "bx", "by"), P(), P(), P("bx", "by", None))
    return jax.shard_map(
        shards, mesh=mesh, in_specs=placed, out_specs=P(None, ("bx", "bz"), "by"), check_vma=False
    )
```

```python
import functools
import math

import jax
import jax.numpy as jnp
from jax import lax
from jax.experimental import pallas as pl
from jax.experimental.pallas import tpu as pltpu
from jax.sharding import PartitionSpec as P

LANES = 128
SUBLANES = 8
TILE = 16
PAD = 8
REACH = 2
COLOR_UNIT = 4096.0
EXTINCTION_UNIT = 2048.0
VMEM_LIMIT = 12 * 2**20

VMEM = pl.BlockSpec(memory_space=pltpu.VMEM)
HBM = pl.BlockSpec(memory_space=pltpu.HBM)


def lane_index():
    return lax.broadcasted_iota(jnp.int32, (SUBLANES, LANES), 1)


def is_odd(axis):
    return jnp.bitwise_and(lax.axis_index(axis), 1) == 1


def swaps(count):
    first = [(i, i ^ 1) for i in range(count)]
    second = [(i, i + 1 if i % 2 else i - 1) for i in range(1, count - 1)]
    return first, second


def faces_kernel(counts, order, density, colors, extinction, padded, ya, yb, xa, xb, za, zb, tables, flags, place, hues, thick, arrived):
    planes, rows, _ = density.shape
    parts = arrived.shape[0] - 3
    step = rows // parts
    copies = [
        pltpu.make_async_copy(
            density.at[:, pl.ds(k * step, step), :],
            padded.at[pl.ds(REACH, planes), pl.ds(PAD + k * step, step), :],
            arrived.at[k],
        )
        for k in range(parts)
    ]
    small = [
        pltpu.make_async_copy(source, target, arrived.at[parts + k])
        for k, (source, target) in enumerate(((order, place), (colors, hues), (extinction, thick)))
    ]
    for copy in copies + small:
        copy.start()
    slot = jnp.right_shift(lane_index(), 2)
    for k in range(parts):
        copies[k].wait()
        for tile in range(step // SUBLANES):
            row = k * step + tile * SUBLANES
            packed = jnp.zeros((SUBLANES, LANES), jnp.float32)
            for z in range(planes):
                plane = padded[REACH + z, PAD + row : PAD + row + SUBLANES, :]
                packed = jnp.where(slot == z, pltpu.roll(plane, (4 * z + REACH) % LANES, 1), packed)
            ya[row : row + SUBLANES, :] = packed
            yb[row : row + SUBLANES, :] = packed
    odd_x, odd_z = is_odd("bx"), is_odd("bz")
    low_x, high_x = PAD, PAD + rows - REACH
    low_z, high_z = REACH, planes
    for out, start in ((xa, jnp.where(odd_x, low_x, high_x)), (xb, jnp.where(odd_x, high_x, low_x))):
        for z in range(planes):
            out[REACH * z : REACH * (z + 1), :] = padded[REACH + z, pl.ds(start, REACH), :]
    for out, start in ((za, jnp.where(odd_z, low_z, high_z)), (zb, jnp.where(odd_z, high_z, low_z))):
        if out is zb and counts["bz"] == 2:
            continue
        for layer in range(REACH):
            out[layer] = padded[start + layer, PAD : PAD + rows, :]
    if counts["bz"] == 2:
        zb[...] = jnp.zeros(zb.shape, jnp.float32)
    for copy in small:
        copy.wait()
    slabs = counts["bz"]
    backward = (place[0, 0, 0] > place[0, 0, slabs - 1]).astype(jnp.float32)
    rank = jnp.bitwise_xor(lax.axis_index("bz"), place[0, 0, 0])
    flags[0] = jnp.full((SUBLANES, LANES), backward, jnp.float32)
    for bit in range(slabs.bit_length() - 1):
        behind = jnp.bitwise_and(jnp.right_shift(rank, bit), 1).astype(jnp.float32)
        flags[1 + bit] = jnp.full((SUBLANES, LANES), behind, jnp.float32)
    color = (hues[...].astype(jnp.float32) * COLOR_UNIT).astype(jnp.int32)
    dense = (thick[...].astype(jnp.float32) * EXTINCTION_UNIT).astype(jnp.int32)
    for k, table in enumerate((color[0:1] * 65536 + color[1:2], color[2:3] * 65536 + dense)):
        for part in range(2):
            tables[2 * k + part] = jnp.broadcast_to(
                table[:, part * LANES : (part + 1) * LANES], (SUBLANES, LANES)
            )


def faces(order, density, colors, extinction, counts):
    planes, rows, cols = density.shape
    shape = lambda *dims: pltpu.VMEM(dims, jnp.float32)
    z_rows = rows if counts["bz"] > 2 else SUBLANES
    face = REACH * rows
    return pl.pallas_call(
        functools.partial(faces_kernel, counts),
        out_shape=(
            shape(planes + 2 * REACH, rows + 2 * PAD, cols),
            shape(face + 16, LANES),
            shape(rows + 8, LANES),
            shape(face + 24, cols),
            shape(rows + 16, cols),
            shape(REACH, rows, cols),
            shape(REACH, z_rows, cols),
            pltpu.VMEM((4, SUBLANES, LANES), jnp.int32),
            shape(counts["bz"].bit_length(), SUBLANES, LANES),
        ),
        in_specs=[HBM] * 4,
        out_specs=(VMEM,) * 9,
        scratch_shapes=[
            pltpu.SMEM(order.shape, jnp.int32),
            pltpu.VMEM(colors.shape, colors.dtype),
            pltpu.VMEM(extinction.shape, extinction.dtype),
            pltpu.SemaphoreType.DMA((7,)),
        ],
        compiler_params=pltpu.CompilerParams(vmem_limit_bytes=VMEM_LIMIT),
        name="faces",
    )(*(pltpu.with_memory_space_constraint(a, pltpu.HBM) for a in (order, density, colors, extinction)))


def half_rows(tile_rows, index, rows, giving):
    block_rows = rows // lax.axis_size("bz")
    half = jnp.bitwise_and(lax.axis_index("bz") + (1 if giving else 0), 1)
    to = pl.multiple_of(index * tile_rows, tile_rows)
    row = (lax.div(to, block_rows) + half) * block_rows + to
    return to, pl.multiple_of(row, tile_rows)


def band_matrix():
    k = jnp.bitwise_and(lax.broadcasted_iota(jnp.int32, (2 * LANES, LANES), 0), LANES - 1)
    gap = k - lax.broadcasted_iota(jnp.int32, (2 * LANES, LANES), 1)
    band = jnp.where(gap == 1, 8.0, jnp.where(gap == -1, -8.0, 0.0))
    band = band + jnp.where(gap == 2, -1.0, jnp.where(gap == -2, 1.0, 0.0))
    return band.astype(jnp.bfloat16)


def slopes_along_y(padded, band, row, planes):
    coarse, fine = [], []
    for z in range(planes):
        plane = padded[REACH + z, pl.ds(PAD + row, TILE), :]
        rounded = plane.astype(jnp.bfloat16)
        coarse.append(rounded)
        fine.append((plane - rounded.astype(jnp.float32)).astype(jnp.bfloat16))
    both = jnp.concatenate([jnp.concatenate(coarse, axis=0), jnp.concatenate(fine, axis=0)], axis=1)
    return jnp.dot(both, band, preferred_element_type=jnp.float32)


def take(tables, first, low, upper):
    found = [
        jnp.take_along_axis(tables[first + k], low, axis=1, mode="promise_in_bounds")
        for k in range(2)
    ]
    return jnp.where(upper, found[1], found[0])


def absorb(padded, material, tables, z, row, clear, scale):
    density = padded[REACH + z, pl.ds(PAD + row, SUBLANES), :]
    label = material[z, pl.ds(row, SUBLANES), :]
    low = jnp.bitwise_and(label, LANES - 1)
    upper = label >= LANES
    rg = take(tables, 0, low, upper)
    be = take(tables, 2, low, upper)
    extinct = jnp.bitwise_and(be, 65535).astype(jnp.float32)
    after = clear * jnp.exp2(extinct * (density * scale))
    stopped = clear - after
    whole = (jnp.right_shift(rg, 16), jnp.bitwise_and(rg, 65535), jnp.right_shift(be, 16))
    return [stopped * part.astype(jnp.float32) for part in whole], after


def shading_at(padded, slope_y, beside, at_edge, z, row):
    at = lambda dz, dx: padded[REACH + z + dz, pl.ds(PAD + row + dx, SUBLANES), :]
    sz = 8.0 * (at(1, 0) - at(-1, 0)) - (at(2, 0) - at(-2, 0))
    sx = 8.0 * (at(0, 1) - at(0, -1)) - (at(0, 2) - at(0, -2))
    outer = pltpu.roll(beside, jnp.bitwise_and(-4 * z - REACH, LANES - 1), 1)
    sy = slope_y + jnp.where(at_edge, outer, 0.0)
    size = sx * sx + sy * sy + sz * sz
    facing = jnp.abs(0.432 * sx + 0.54 * sy + 0.576 * sz)
    return 0.1 + facing * lax.rsqrt(jnp.maximum(size, 36.0))


def edge_lanes():
    lane = lane_index()
    return jnp.logical_or(lane < REACH, lane >= LANES - REACH)


def scale_of(total_planes):
    return -3.0 * math.log2(math.e) / (EXTINCTION_UNIT * total_planes)


def local_give_kernel(total_planes, padded, material, tables, flags, lit, slope_y, through):
    planes, rows, _ = material.shape
    backward = jnp.max(flags[0]) > 0.5
    band = band_matrix()
    scale = scale_of(total_planes)

    def tile(index, carry):
        to, row = half_rows(TILE, index, rows, True)
        slopes = slopes_along_y(padded, band, row, planes)
        for z in range(planes):
            slope_y[z, pl.ds(to, TILE), :] = slopes[TILE * z : TILE * (z + 1)]
        for part in range(0, TILE, SUBLANES):
            clear = jnp.ones((SUBLANES, LANES), jnp.float32)
            for visit in range(planes):
                z = jnp.where(backward, planes - 1 - visit, visit)
                light, clear = absorb(padded, material, tables, z, row + part, clear, scale)
                for c in range(3):
                    lit[c, z, pl.ds(to + part, SUBLANES), :] = light[c]
            through[pl.ds(to + part, SUBLANES), :] = clear
        return carry

    lax.fori_loop(0, rows // 2 // TILE, tile, 0)


def local_give(padded, material, tables, flags, total_planes):
    planes, rows, cols = material.shape
    shape = lambda *dims: pltpu.VMEM(dims, jnp.float32)
    return pl.pallas_call(
        functools.partial(local_give_kernel, total_planes),
        out_shape=(
            shape(3, planes, rows // 2, cols),
            shape(planes, rows // 2, cols),
            shape(rows // 2, cols),
        ),
        in_specs=[VMEM] * 4,
        out_specs=(VMEM,) * 3,
        compiler_params=pltpu.CompilerParams(vmem_limit_bytes=VMEM_LIMIT),
        cost_estimate=pl.CostEstimate(
            flops=20 * planes * rows * cols,
            bytes_accessed=2**22,
            transcendentals=planes * rows * cols,
        ),
        name="local_give",
    )(padded, material, tables, flags)


def put_halo(padded, xa, xb, za, zb, ya, yb, edge, planes, rows):
    odd_x, odd_y, odd_z = is_odd("bx"), is_odd("by"), is_odd("bz")
    for z in range(planes):
        first, second = xa[REACH * z : REACH * (z + 1), :], xb[REACH * z : REACH * (z + 1), :]
        padded[REACH + z, PAD - REACH : PAD, :] = jnp.where(odd_x, first, second)
        padded[REACH + z, PAD + rows : PAD + rows + REACH, :] = jnp.where(odd_x, second, first)
    for layer in range(REACH):
        first = za[layer]
        second = zb[layer] if zb.shape == za.shape else jnp.zeros_like(first)
        padded[layer, PAD : PAD + rows, :] = jnp.where(odd_z, first, second)
        padded[REACH + planes + layer, PAD : PAD + rows, :] = jnp.where(odd_z, second, first)
    side = jnp.bitwise_and(lane_index(), 3)
    for row in range(0, rows, SUBLANES):
        first, second = ya[row : row + SUBLANES, :], yb[row : row + SUBLANES, :]
        near = jnp.where((side < 2) == odd_y, first, second)
        ahead1, ahead2 = pltpu.roll(near, LANES - 1, 1), pltpu.roll(near, LANES - 2, 1)
        behind1, behind2 = pltpu.roll(near, 1, 1), pltpu.roll(near, 2, 1)
        edge[row : row + SUBLANES, :] = jnp.where(
            side == 0,
            -ahead2,
            jnp.where(
                side == 1,
                8.0 * ahead1 - ahead2,
                jnp.where(side == 2, behind2 - 8.0 * behind1, behind2),
            ),
        )


def shade_give_kernel(padded_in, xa, xb, za, zb, ya, yb, lit, slope_y, through, padded, edge, give):
    _, planes, half, _ = lit.shape
    rows = 2 * half
    del padded_in
    put_halo(padded, xa, xb, za, zb, ya, yb, edge, planes, rows)
    at_edge = edge_lanes()

    def tile(index, carry):
        to, row = half_rows(TILE, index, rows, True)
        for part in range(0, TILE, SUBLANES):
            beside = edge[pl.ds(row + part, SUBLANES), :]
            place = pl.ds(to + part, SUBLANES)
            sums = [jnp.zeros((SUBLANES, LANES), jnp.float32) for _ in range(3)]
            for z in range(planes):
                shading = shading_at(padded, slope_y[z, place, :], beside, at_edge, z, row + part)
                for c in range(3):
                    sums[c] = sums[c] + shading * lit[c, z, place, :]
            for c in range(3):
                give[c, place, :] = sums[c] * (1.0 / COLOR_UNIT)
            give[3, place, :] = through[place, :]
        return carry

    lax.fori_loop(0, half // TILE, tile, 0)


def shade_give(padded, halos, lit, slope_y, through):
    _, _, half, cols = lit.shape
    shape = lambda *dims: pltpu.VMEM(dims, jnp.float32)
    return pl.pallas_call(
        shade_give_kernel,
        out_shape=(shape(*padded.shape), shape(2 * half, LANES), shape(4, half, cols)),
        in_specs=[VMEM] * 10,
        out_specs=(VMEM,) * 3,
        input_output_aliases={0: 0},
        compiler_params=pltpu.CompilerParams(vmem_limit_bytes=VMEM_LIMIT),
        name="shade_give",
    )(padded, *halos, lit, slope_y, through)


def keep_kernel(total_planes, padded, edge, material, tables, flags, keep, slope_y):
    planes, rows, _ = material.shape
    backward = jnp.max(flags[0]) > 0.5
    band = band_matrix()
    scale = scale_of(total_planes)
    at_edge = edge_lanes()

    def tile(index, carry):
        to, row = half_rows(TILE, index, rows, False)
        slope_y[...] = slopes_along_y(padded, band, row, planes).reshape(planes, TILE, LANES)
        for part in range(0, TILE, SUBLANES):
            beside = edge[pl.ds(row + part, SUBLANES), :]
            place = pl.ds(to + part, SUBLANES)
            clear = jnp.ones((SUBLANES, LANES), jnp.float32)
            sums = [jnp.zeros((SUBLANES, LANES), jnp.float32) for _ in range(3)]
            for visit in range(planes):
                z = jnp.where(backward, planes - 1 - visit, visit)
                slope = slope_y[z, part : part + SUBLANES, :]
                light, clear = absorb(padded, material, tables, z, row + part, clear, scale)
                shading = shading_at(padded, slope, beside, at_edge, z, row + part)
                for c in range(3):
                    sums[c] = sums[c] + shading * light[c]
            for c in range(3):
                keep[c, place, :] = sums[c] * (1.0 / COLOR_UNIT)
            keep[3, place, :] = clear
        return carry

    lax.fori_loop(0, rows // 2 // TILE, tile, 0)


def shade_keep(padded, edge, material, tables, flags, total_planes):
    planes, rows, cols = material.shape
    return pl.pallas_call(
        functools.partial(keep_kernel, total_planes),
        out_shape=pltpu.VMEM((4, rows // 2, cols), jnp.float32),
        in_specs=[VMEM] * 5,
        out_specs=VMEM,
        scratch_shapes=[pltpu.VMEM((planes, TILE, LANES), jnp.float32)],
        compiler_params=pltpu.CompilerParams(vmem_limit_bytes=VMEM_LIMIT),
        cost_estimate=pl.CostEstimate(
            flops=40 * planes * rows * cols,
            bytes_accessed=2**22,
            transcendentals=planes * rows * cols,
        ),
        name="keep",
    )(padded, edge, material, tables, flags)


def blend_kernel(bit, last, flags, mine, other, out):
    clear_mine, clear_other = mine[3], other[3]
    behind = jnp.broadcast_to(flags[1 + bit, 0:1, :], clear_mine.shape) > 0.5
    clear = jnp.where(behind, clear_other, clear_mine)
    for c in range(3):
        front = jnp.where(behind, other[c], mine[c])
        back = jnp.where(behind, mine[c], other[c])
        out[c] = front + clear * back
    product = clear_mine * clear_other
    out[3] = 1.0 - product if last else product


def blend(flags, mine, other, bit, last):
    return pl.pallas_call(
        functools.partial(blend_kernel, bit, last),
        out_shape=jax.ShapeDtypeStruct(mine.shape, jnp.float32),
        in_specs=[VMEM] * 3,
        out_specs=VMEM,
        compiler_params=pltpu.CompilerParams(vmem_limit_bytes=VMEM_LIMIT),
        name="blend",
    )(flags, mine, other)


def shards(density, material, color_table, extinction_table, order):
    planes, rows, cols = density.shape
    counts = {axis: lax.axis_size(axis) for axis in ("bx", "by", "bz")}
    slabs = counts["bz"]
    padded, ya, yb, xa, xb, za, zb, tables, flags = faces(
        order, density, color_table, extinction_table, counts
    )
    pairs = {axis: swaps(counts[axis]) for axis in counts}
    xa = lax.ppermute(xa, "bx", pairs["bx"][0])
    xb = lax.ppermute(xb, "bx", pairs["bx"][1])
    za = lax.ppermute(za, "bz", pairs["bz"][0])
    if slabs > 2:
        zb = lax.ppermute(zb, "bz", pairs["bz"][1])
    ya = lax.ppermute(ya, "by", pairs["by"][0])
    yb = lax.ppermute(yb, "by", pairs["by"][1])
    lit, slope_y, through = local_give(padded, material, tables, flags, planes * slabs)
    halos = (xa, xb, za, zb, ya, yb)
    padded, edge, give = shade_give(padded, halos, lit, slope_y, through)
    keep = shade_keep(padded, edge, material, tables, flags, planes * slabs)
    block_rows = rows // slabs
    levels = slabs.bit_length() - 1
    my_slab = lax.axis_index("bz")
    for bit in range(levels):
        flip = [(i, i ^ (1 << bit)) for i in range(slabs)]
        received = lax.ppermute(give, "bz", flip)
        holding = blend(flags, keep, received, bit, bit == levels - 1)
        if bit < levels - 1:
            paired = holding.reshape(4, -1, 2, block_rows, cols)
            half = jnp.bitwise_and(jnp.right_shift(my_slab, bit + 1), 1)
            take = lambda which: lax.dynamic_index_in_dim(paired, which, 2, keepdims=False)
            keep, give = (take(which).reshape(4, -1, cols) for which in (half, 1 - half))
    return holding


def solution(mesh):
    placed = (P("bz", "bx", "by"), P("bz", "bx", "by"), P(), P(), P("bx", "by", None))
    return jax.shard_map(
        shards, mesh=mesh, in_specs=placed, out_specs=P(None, ("bx", "bz"), "by"), check_vma=False
    )
```

```python
import functools
import math

import jax
import jax.numpy as jnp
from jax import lax
from jax.experimental import pallas as pl
from jax.experimental.pallas import tpu as pltpu
from jax.sharding import PartitionSpec as P

LANES = 128
SUBLANES = 8
TILE = 16
PAD = 8
REACH = 2
COLOR_UNIT = 4096.0
EXTINCTION_UNIT = 2048.0
VMEM_LIMIT = 12 * 2**20

VMEM = pl.BlockSpec(memory_space=pltpu.VMEM)
HBM = pl.BlockSpec(memory_space=pltpu.HBM)


def lane_index():
    return lax.broadcasted_iota(jnp.int32, (SUBLANES, LANES), 1)


def is_odd(axis):
    return jnp.bitwise_and(lax.axis_index(axis), 1) == 1


def swaps(count):
    first = [(i, i ^ 1) for i in range(count)]
    second = [(i, i + 1 if i % 2 else i - 1) for i in range(1, count - 1)]
    return first, second


def x_face(out, source, start, planes):
    for z in range(planes):
        out[REACH * z : REACH * (z + 1), :] = source(z, start)


def early_kernel(counts, order, density, colors, extinction, xa, za, zb, tables, flags, place, hues, thick, rows_x, arrived):
    planes, rows, _ = density.shape
    odd_x, odd_z, top = is_odd("bx"), is_odd("bz"), planes - REACH
    ends = [(za, jnp.where(odd_z, 0, top))]
    if counts["bz"] > 2:
        ends.append((zb, jnp.where(odd_z, top, 0)))
    low_x = pl.multiple_of(jnp.where(odd_x, 0, rows - SUBLANES), SUBLANES)
    pairs = [(density.at[:, pl.ds(low_x, SUBLANES), :], rows_x)]
    pairs += [(density.at[pl.ds(start, REACH)], out) for out, start in ends]
    pairs += [(order, place), (colors, hues), (extinction, thick)]
    copies = [
        pltpu.make_async_copy(source, target, arrived.at[k])
        for k, (source, target) in enumerate(pairs)
    ]
    for copy in copies:
        copy.start()
    for copy in copies[-3:]:
        copy.wait()
    slabs = counts["bz"]
    backward = (place[0, 0, 0] > place[0, 0, slabs - 1]).astype(jnp.float32)
    rank = jnp.bitwise_xor(lax.axis_index("bz"), place[0, 0, 0])
    flags[0] = jnp.full((SUBLANES, LANES), backward, jnp.float32)
    for bit in range(slabs.bit_length() - 1):
        behind = jnp.bitwise_and(jnp.right_shift(rank, bit), 1).astype(jnp.float32)
        flags[1 + bit] = jnp.full((SUBLANES, LANES), behind, jnp.float32)
    color = (hues[...].astype(jnp.float32) * COLOR_UNIT).astype(jnp.int32)
    dense = (thick[...].astype(jnp.float32) * EXTINCTION_UNIT).astype(jnp.int32)
    for k, table in enumerate((color[0:1] * 65536 + color[1:2], color[2:3] * 65536 + dense)):
        for part in range(2):
            tables[2 * k + part] = jnp.broadcast_to(
                table[:, part * LANES : (part + 1) * LANES], (SUBLANES, LANES)
            )
    if counts["bz"] == 2:
        zb[...] = jnp.zeros(zb.shape, jnp.float32)
    for copy in copies[:-3]:
        copy.wait()
    start = jnp.where(odd_x, 0, SUBLANES - REACH)
    x_face(xa, lambda z, at: rows_x[z, pl.ds(at, REACH), :], start, planes)


def pack_kernel(density, padded, ya, yb, xb, arrived):
    planes, rows, _ = density.shape
    whole = pltpu.make_async_copy(
        density, padded.at[pl.ds(REACH, planes), pl.ds(PAD, rows), :], arrived
    )
    whole.start()
    start = jnp.where(is_odd("bx"), rows - REACH, 0)
    x_face(xb, lambda z, at: density[z, pl.ds(at, REACH), :], start, planes)
    slot = jnp.right_shift(lane_index(), 2)
    for row in range(0, rows, SUBLANES):
        packed = jnp.zeros((SUBLANES, LANES), jnp.float32)
        for z in range(planes):
            plane = density[z, row : row + SUBLANES, :]
            packed = jnp.where(slot == z, pltpu.roll(plane, (4 * z + REACH) % LANES, 1), packed)
        ya[row : row + SUBLANES, :] = packed
        yb[row : row + SUBLANES, :] = packed
    whole.wait()


def faces(order, density, colors, extinction, counts):
    planes, rows, cols = density.shape
    shape = lambda *dims: pltpu.VMEM(dims, jnp.float32)
    z_rows = rows if counts["bz"] > 2 else SUBLANES
    face = REACH * rows
    params = pltpu.CompilerParams(vmem_limit_bytes=VMEM_LIMIT)
    fixed = [
        pltpu.with_memory_space_constraint(a, pltpu.HBM)
        for a in (order, density, colors, extinction)
    ]
    xa, za, zb, tables, flags = pl.pallas_call(
        functools.partial(early_kernel, counts),
        out_shape=(
            shape(face + 24, cols),
            shape(REACH, rows, cols),
            shape(REACH, z_rows, cols),
            pltpu.VMEM((4, SUBLANES, LANES), jnp.int32),
            shape(counts["bz"].bit_length(), SUBLANES, LANES),
        ),
        in_specs=[HBM] * 4,
        out_specs=(VMEM,) * 5,
        scratch_shapes=[
            pltpu.SMEM(order.shape, jnp.int32),
            pltpu.VMEM(colors.shape, colors.dtype),
            pltpu.VMEM(extinction.shape, extinction.dtype),
            pltpu.VMEM((planes, SUBLANES, cols), jnp.float32),
            pltpu.SemaphoreType.DMA((6,)),
        ],
        compiler_params=params,
        name="early",
    )(*fixed)
    padded, ya, yb, xb = pl.pallas_call(
        pack_kernel,
        out_shape=(
            shape(planes + 2 * REACH, rows + 2 * PAD, cols),
            shape(rows + 24, LANES),
            shape(rows + 8, LANES),
            shape(rows + 16, cols),
        ),
        in_specs=[VMEM],
        out_specs=(VMEM,) * 4,
        scratch_shapes=[pltpu.SemaphoreType.DMA],
        compiler_params=params,
        name="pack",
    )(density)
    return padded, ya, yb, xa, xb, za, zb, tables, flags


def half_rows(tile_rows, index, rows, giving):
    block_rows = rows // lax.axis_size("bz")
    half = jnp.bitwise_and(lax.axis_index("bz") + (1 if giving else 0), 1)
    to = pl.multiple_of(index * tile_rows, tile_rows)
    row = (lax.div(to, block_rows) + half) * block_rows + to
    return to, pl.multiple_of(row, tile_rows)


def band_matrix():
    k = jnp.bitwise_and(lax.broadcasted_iota(jnp.int32, (2 * LANES, LANES), 0), LANES - 1)
    gap = k - lax.broadcasted_iota(jnp.int32, (2 * LANES, LANES), 1)
    band = jnp.where(gap == 1, 8.0, jnp.where(gap == -1, -8.0, 0.0))
    band = band + jnp.where(gap == 2, -1.0, jnp.where(gap == -2, 1.0, 0.0))
    return band.astype(jnp.bfloat16)


def slopes_along_y(padded, band, row, planes):
    coarse, fine = [], []
    for z in range(planes):
        plane = padded[REACH + z, pl.ds(PAD + row, TILE), :]
        rounded = plane.astype(jnp.bfloat16)
        coarse.append(rounded)
        fine.append((plane - rounded.astype(jnp.float32)).astype(jnp.bfloat16))
    both = jnp.concatenate([jnp.concatenate(coarse, axis=0), jnp.concatenate(fine, axis=0)], axis=1)
    return jnp.dot(both, band, preferred_element_type=jnp.float32)


def take(tables, first, low, upper):
    found = [
        jnp.take_along_axis(tables[first + k], low, axis=1, mode="promise_in_bounds")
        for k in range(2)
    ]
    return jnp.where(upper, found[1], found[0])


def absorb(padded, material, tables, z, row, clear, scale):
    density = padded[REACH + z, pl.ds(PAD + row, SUBLANES), :]
    label = material[z, pl.ds(row, SUBLANES), :]
    low = jnp.bitwise_and(label, LANES - 1)
    upper = label >= LANES
    rg = take(tables, 0, low, upper)
    be = take(tables, 2, low, upper)
    extinct = jnp.bitwise_and(be, 65535).astype(jnp.float32)
    after = clear * jnp.exp2(extinct * (density * scale))
    stopped = clear - after
    whole = (jnp.right_shift(rg, 16), jnp.bitwise_and(rg, 65535), jnp.right_shift(be, 16))
    return [stopped * part.astype(jnp.float32) for part in whole], after


def shading_at(padded, slope_y, beside, at_edge, z, row):
    at = lambda dz, dx: padded[REACH + z + dz, pl.ds(PAD + row + dx, SUBLANES), :]
    sz = 8.0 * (at(1, 0) - at(-1, 0)) - (at(2, 0) - at(-2, 0))
    sx = 8.0 * (at(0, 1) - at(0, -1)) - (at(0, 2) - at(0, -2))
    outer = pltpu.roll(beside, jnp.bitwise_and(-4 * z - REACH, LANES - 1), 1)
    sy = slope_y + jnp.where(at_edge, outer, 0.0)
    size = sx * sx + sy * sy + sz * sz
    facing = jnp.abs(0.432 * sx + 0.54 * sy + 0.576 * sz)
    return 0.1 + facing * lax.rsqrt(jnp.maximum(size, 36.0))


def edge_lanes():
    lane = lane_index()
    return jnp.logical_or(lane < REACH, lane >= LANES - REACH)


def scale_of(total_planes):
    return -3.0 * math.log2(math.e) / (EXTINCTION_UNIT * total_planes)


def local_give_kernel(total_planes, padded, material, tables, flags, lit, slope_y, through):
    planes, rows, _ = material.shape
    backward = jnp.max(flags[0]) > 0.5
    band = band_matrix()
    scale = scale_of(total_planes)

    def tile(index, carry):
        to, row = half_rows(TILE, index, rows, True)
        slopes = slopes_along_y(padded, band, row, planes)
        for z in range(planes):
            slope_y[z, pl.ds(to, TILE), :] = slopes[TILE * z : TILE * (z + 1)]
        for part in range(0, TILE, SUBLANES):
            clear = jnp.ones((SUBLANES, LANES), jnp.float32)
            for visit in range(planes):
                z = jnp.where(backward, planes - 1 - visit, visit)
                light, clear = absorb(padded, material, tables, z, row + part, clear, scale)
                for c in range(3):
                    lit[c, z, pl.ds(to + part, SUBLANES), :] = light[c]
            through[pl.ds(to + part, SUBLANES), :] = clear
        return carry

    lax.fori_loop(0, rows // 2 // TILE, tile, 0)


def local_give(padded, material, tables, flags, total_planes):
    planes, rows, cols = material.shape
    shape = lambda *dims: pltpu.VMEM(dims, jnp.float32)
    return pl.pallas_call(
        functools.partial(local_give_kernel, total_planes),
        out_shape=(
            shape(3, planes, rows // 2, cols),
            shape(planes, rows // 2, cols),
            shape(rows // 2, cols),
        ),
        in_specs=[VMEM] * 4,
        out_specs=(VMEM,) * 3,
        compiler_params=pltpu.CompilerParams(vmem_limit_bytes=VMEM_LIMIT),
        cost_estimate=pl.CostEstimate(
            flops=20 * planes * rows * cols,
            bytes_accessed=2**22,
            transcendentals=planes * rows * cols,
        ),
        name="local_give",
    )(padded, material, tables, flags)


def put_halo(padded, xa, xb, za, zb, ya, yb, edge, planes, rows):
    odd_x, odd_y, odd_z = is_odd("bx"), is_odd("by"), is_odd("bz")
    for z in range(planes):
        first, second = xa[REACH * z : REACH * (z + 1), :], xb[REACH * z : REACH * (z + 1), :]
        padded[REACH + z, PAD - REACH : PAD, :] = jnp.where(odd_x, first, second)
        padded[REACH + z, PAD + rows : PAD + rows + REACH, :] = jnp.where(odd_x, second, first)
    for layer in range(REACH):
        first = za[layer]
        second = zb[layer] if zb.shape == za.shape else jnp.zeros_like(first)
        padded[layer, PAD : PAD + rows, :] = jnp.where(odd_z, first, second)
        padded[REACH + planes + layer, PAD : PAD + rows, :] = jnp.where(odd_z, second, first)
    side = jnp.bitwise_and(lane_index(), 3)
    for row in range(0, rows, SUBLANES):
        first, second = ya[row : row + SUBLANES, :], yb[row : row + SUBLANES, :]
        near = jnp.where((side < 2) == odd_y, first, second)
        ahead1, ahead2 = pltpu.roll(near, LANES - 1, 1), pltpu.roll(near, LANES - 2, 1)
        behind1, behind2 = pltpu.roll(near, 1, 1), pltpu.roll(near, 2, 1)
        edge[row : row + SUBLANES, :] = jnp.where(
            side == 0,
            -ahead2,
            jnp.where(
                side == 1,
                8.0 * ahead1 - ahead2,
                jnp.where(side == 2, behind2 - 8.0 * behind1, behind2),
            ),
        )


def shade_give_kernel(padded_in, xa, xb, za, zb, ya, yb, lit, slope_y, through, padded, edge, give):
    _, planes, half, _ = lit.shape
    rows = 2 * half
    del padded_in
    put_halo(padded, xa, xb, za, zb, ya, yb, edge, planes, rows)
    at_edge = edge_lanes()

    def tile(index, carry):
        for step in range(2 * (TILE // SUBLANES)):
            to, row = half_rows(TILE, 2 * index + step // 2, rows, True)
            part = step % 2 * SUBLANES
            beside = edge[pl.ds(row + part, SUBLANES), :]
            place = pl.ds(to + part, SUBLANES)
            sums = [jnp.zeros((SUBLANES, LANES), jnp.float32) for _ in range(3)]
            for z in range(planes):
                shading = shading_at(padded, slope_y[z, place, :], beside, at_edge, z, row + part)
                for c in range(3):
                    sums[c] = sums[c] + shading * lit[c, z, place, :]
            for c in range(3):
                give[c, place, :] = sums[c] * (1.0 / COLOR_UNIT)
            give[3, place, :] = through[place, :]
        return carry

    lax.fori_loop(0, half // TILE // 2, tile, 0)


def shade_give(padded, halos, lit, slope_y, through):
    _, _, half, cols = lit.shape
    shape = lambda *dims: pltpu.VMEM(dims, jnp.float32)
    return pl.pallas_call(
        shade_give_kernel,
        out_shape=(shape(*padded.shape), shape(2 * half, LANES), shape(4, half, cols)),
        in_specs=[VMEM] * 10,
        out_specs=(VMEM,) * 3,
        input_output_aliases={0: 0},
        compiler_params=pltpu.CompilerParams(vmem_limit_bytes=VMEM_LIMIT),
        name="shade_give",
    )(padded, *halos, lit, slope_y, through)


def keep_kernel(total_planes, padded, edge, material, tables, flags, keep, slope_y):
    planes, rows, _ = material.shape
    backward = jnp.max(flags[0]) > 0.5
    band = band_matrix()
    scale = scale_of(total_planes)
    at_edge = edge_lanes()

    def tile(index, carry):
        to, row = half_rows(TILE, index, rows, False)
        slope_y[...] = slopes_along_y(padded, band, row, planes).reshape(planes, TILE, LANES)
        for part in range(0, TILE, SUBLANES):
            beside = edge[pl.ds(row + part, SUBLANES), :]
            place = pl.ds(to + part, SUBLANES)
            clear = jnp.ones((SUBLANES, LANES), jnp.float32)
            sums = [jnp.zeros((SUBLANES, LANES), jnp.float32) for _ in range(3)]
            for visit in range(planes):
                z = jnp.where(backward, planes - 1 - visit, visit)
                slope = slope_y[z, part : part + SUBLANES, :]
                light, clear = absorb(padded, material, tables, z, row + part, clear, scale)
                shading = shading_at(padded, slope, beside, at_edge, z, row + part)
                for c in range(3):
                    sums[c] = sums[c] + shading * light[c]
            for c in range(3):
                keep[c, place, :] = sums[c] * (1.0 / COLOR_UNIT)
            keep[3, place, :] = clear
        return carry

    lax.fori_loop(0, rows // 2 // TILE, tile, 0)


def shade_keep(padded, edge, material, tables, flags, total_planes):
    planes, rows, cols = material.shape
    return pl.pallas_call(
        functools.partial(keep_kernel, total_planes),
        out_shape=pltpu.VMEM((4, rows // 2, cols), jnp.float32),
        in_specs=[VMEM] * 5,
        out_specs=VMEM,
        scratch_shapes=[pltpu.VMEM((planes, TILE, LANES), jnp.float32)],
        compiler_params=pltpu.CompilerParams(vmem_limit_bytes=VMEM_LIMIT),
        cost_estimate=pl.CostEstimate(
            flops=40 * planes * rows * cols,
            bytes_accessed=2**22,
            transcendentals=planes * rows * cols,
        ),
        name="keep",
    )(padded, edge, material, tables, flags)


def blend_kernel(bit, last, flags, mine, other, out):
    clear_mine, clear_other = mine[3], other[3]
    behind = jnp.broadcast_to(flags[1 + bit, 0:1, :], clear_mine.shape) > 0.5
    clear = jnp.where(behind, clear_other, clear_mine)
    for c in range(3):
        front = jnp.where(behind, other[c], mine[c])
        back = jnp.where(behind, mine[c], other[c])
        out[c] = front + clear * back
    product = clear_mine * clear_other
    out[3] = 1.0 - product if last else product


def blend(flags, mine, other, bit, last):
    return pl.pallas_call(
        functools.partial(blend_kernel, bit, last),
        out_shape=jax.ShapeDtypeStruct(mine.shape, jnp.float32),
        in_specs=[VMEM] * 3,
        out_specs=VMEM,
        compiler_params=pltpu.CompilerParams(vmem_limit_bytes=VMEM_LIMIT),
        name="blend",
    )(flags, mine, other)


def shards(density, material, color_table, extinction_table, order):
    planes, rows, cols = density.shape
    counts = {axis: lax.axis_size(axis) for axis in ("bx", "by", "bz")}
    slabs = counts["bz"]
    padded, ya, yb, xa, xb, za, zb, tables, flags = faces(
        order, density, color_table, extinction_table, counts
    )
    pairs = {axis: swaps(counts[axis]) for axis in counts}
    xa = lax.ppermute(xa, "bx", pairs["bx"][0])
    xb = lax.ppermute(xb, "bx", pairs["bx"][1])
    za = lax.ppermute(za, "bz", pairs["bz"][0])
    if slabs > 2:
        zb = lax.ppermute(zb, "bz", pairs["bz"][1])
    ya = lax.ppermute(ya, "by", pairs["by"][0])
    yb = lax.ppermute(yb, "by", pairs["by"][1])
    lit, slope_y, through = local_give(padded, material, tables, flags, planes * slabs)
    halos = (xa, xb, za, zb, ya, yb)
    padded, edge, give = shade_give(padded, halos, lit, slope_y, through)
    keep = shade_keep(padded, edge, material, tables, flags, planes * slabs)
    block_rows = rows // slabs
    levels = slabs.bit_length() - 1
    my_slab = lax.axis_index("bz")
    for bit in range(levels):
        flip = [(i, i ^ (1 << bit)) for i in range(slabs)]
        received = lax.ppermute(give, "bz", flip)
        holding = blend(flags, keep, received, bit, bit == levels - 1)
        if bit < levels - 1:
            paired = holding.reshape(4, -1, 2, block_rows, cols)
            half = jnp.bitwise_and(jnp.right_shift(my_slab, bit + 1), 1)
            take = lambda which: lax.dynamic_index_in_dim(paired, which, 2, keepdims=False)
            keep, give = (take(which).reshape(4, -1, cols) for which in (half, 1 - half))
    return holding


def solution(mesh):
    placed = (P("bz", "bx", "by"), P("bz", "bx", "by"), P(), P(), P("bx", "by", None))
    return jax.shard_map(
        shards, mesh=mesh, in_specs=placed, out_specs=P(None, ("bx", "bz"), "by"), check_vma=False
    )
```

```python
import functools
import math

import jax
import jax.numpy as jnp
from jax import lax
from jax.experimental import pallas as pl
from jax.experimental.pallas import tpu as pltpu
from jax.sharding import PartitionSpec as P

LANES = 128
SUBLANES = 8
TILE = 16
PAD = 8
REACH = 2
COLOR_UNIT = 4096.0
EXTINCTION_UNIT = 2048.0
VMEM_LIMIT = 12 * 2**20

VMEM = pl.BlockSpec(memory_space=pltpu.VMEM)
HBM = pl.BlockSpec(memory_space=pltpu.HBM)


def lane_index():
    return lax.broadcasted_iota(jnp.int32, (SUBLANES, LANES), 1)


def is_odd(axis):
    return jnp.bitwise_and(lax.axis_index(axis), 1) == 1


def swaps(count):
    first = [(i, i ^ 1) for i in range(count)]
    second = [(i, i + 1 if i % 2 else i - 1) for i in range(1, count - 1)]
    return first, second


def x_face(out, source, start, planes):
    for z in range(planes):
        out[REACH * z : REACH * (z + 1), :] = source(z, start)


def early_kernel(counts, order, density, colors, extinction, xa, za, zb, tables, flags, place, hues, thick, rows_x, arrived):
    planes, rows, _ = density.shape
    odd_x, odd_z, top = is_odd("bx"), is_odd("bz"), planes - REACH
    ends = [(za, jnp.where(odd_z, 0, top))]
    if counts["bz"] > 2:
        ends.append((zb, jnp.where(odd_z, top, 0)))
    low_x = pl.multiple_of(jnp.where(odd_x, 0, rows - SUBLANES), SUBLANES)
    pairs = [(density.at[:, pl.ds(low_x, SUBLANES), :], rows_x)]
    pairs += [(density.at[pl.ds(start, REACH)], out) for out, start in ends]
    pairs += [(order, place), (colors, hues), (extinction, thick)]
    copies = [
        pltpu.make_async_copy(source, target, arrived.at[k])
        for k, (source, target) in enumerate(pairs)
    ]
    for copy in copies:
        copy.start()
    for copy in copies[-3:]:
        copy.wait()
    slabs = counts["bz"]
    backward = (place[0, 0, 0] > place[0, 0, slabs - 1]).astype(jnp.float32)
    rank = jnp.bitwise_xor(lax.axis_index("bz"), place[0, 0, 0])
    flags[0] = jnp.full((SUBLANES, LANES), backward, jnp.float32)
    for bit in range(slabs.bit_length() - 1):
        behind = jnp.bitwise_and(jnp.right_shift(rank, bit), 1).astype(jnp.float32)
        flags[1 + bit] = jnp.full((SUBLANES, LANES), behind, jnp.float32)
    color = (hues[...].astype(jnp.float32) * COLOR_UNIT).astype(jnp.int32)
    dense = (thick[...].astype(jnp.float32) * EXTINCTION_UNIT).astype(jnp.int32)
    for k, table in enumerate((color[0:1] * 65536 + color[1:2], color[2:3] * 65536 + dense)):
        for part in range(2):
            tables[2 * k + part] = jnp.broadcast_to(
                table[:, part * LANES : (part + 1) * LANES], (SUBLANES, LANES)
            )
    if counts["bz"] == 2:
        zb[...] = jnp.zeros(zb.shape, jnp.float32)
    for copy in copies[:-3]:
        copy.wait()
    start = jnp.where(odd_x, 0, SUBLANES - REACH)
    x_face(xa, lambda z, at: rows_x[z, pl.ds(at, REACH), :], start, planes)


def pack_kernel(density, padded, ya, yb, xb, columns, arrived):
    planes, rows, _ = density.shape
    whole = pltpu.make_async_copy(
        density, padded.at[pl.ds(REACH, planes), pl.ds(PAD, rows), :], arrived
    )
    whole.start()
    start = jnp.where(is_odd("bx"), rows - REACH, 0)
    x_face(xb, lambda z, at: density[z, pl.ds(at, REACH), :], start, planes)
    slot = jnp.right_shift(lane_index(), 2)
    for row in range(0, rows, SUBLANES):
        packed = jnp.zeros((SUBLANES, LANES), jnp.float32)
        for z in range(planes):
            plane = density[z, row : row + SUBLANES, :]
            packed = jnp.where(slot == z, pltpu.roll(plane, (4 * z + REACH) % LANES, 1), packed)
        columns[row : row + SUBLANES, :] = packed
    side = jnp.bitwise_and(lane_index(), 3)
    odd_y = is_odd("by")
    for row in range(0, rows // 2, SUBLANES):
        upper = columns[row : row + SUBLANES, :]
        lower = pltpu.roll(columns[rows // 2 + row : rows // 2 + row + SUBLANES, :], 2, 1)
        high_face = jnp.where(side < 2, upper, lower)
        lower = pltpu.roll(lower, LANES - 4, 1)
        low_face = jnp.where(side < 2, lower, upper)
        ya[row : row + SUBLANES, :] = jnp.where(odd_y, low_face, high_face)
        yb[row : row + SUBLANES, :] = jnp.where(odd_y, high_face, low_face)
    whole.wait()


def faces(order, density, colors, extinction, counts):
    planes, rows, cols = density.shape
    shape = lambda *dims: pltpu.VMEM(dims, jnp.float32)
    z_rows = rows if counts["bz"] > 2 else SUBLANES
    face = REACH * rows
    size = max(REACH * planes, rows // 2)
    params = pltpu.CompilerParams(vmem_limit_bytes=VMEM_LIMIT)
    fixed = [
        pltpu.with_memory_space_constraint(a, pltpu.HBM)
        for a in (order, density, colors, extinction)
    ]
    xa, za, zb, tables, flags = pl.pallas_call(
        functools.partial(early_kernel, counts),
        out_shape=(
            shape(face + 24, cols),
            shape(REACH, rows, cols),
            shape(REACH, z_rows, cols),
            pltpu.VMEM((4, SUBLANES, LANES), jnp.int32),
            shape(counts["bz"].bit_length(), SUBLANES, LANES),
        ),
        in_specs=[HBM] * 4,
        out_specs=(VMEM,) * 5,
        scratch_shapes=[
            pltpu.SMEM(order.shape, jnp.int32),
            pltpu.VMEM(colors.shape, colors.dtype),
            pltpu.VMEM(extinction.shape, extinction.dtype),
            pltpu.VMEM((planes, SUBLANES, cols), jnp.float32),
            pltpu.SemaphoreType.DMA((6,)),
        ],
        compiler_params=params,
        name="early",
    )(*fixed)
    padded, ya, yb, xb = pl.pallas_call(
        pack_kernel,
        out_shape=(
            shape(planes + 2 * REACH, rows + 2 * PAD, cols),
            shape(size + 16, LANES),
            shape(size, LANES),
            shape(size + 8, cols),
        ),
        in_specs=[VMEM],
        out_specs=(VMEM,) * 4,
        scratch_shapes=[pltpu.VMEM((rows, LANES), jnp.float32), pltpu.SemaphoreType.DMA],
        compiler_params=params,
        name="pack",
    )(density)
    return padded, ya, yb, xa, xb, za, zb, tables, flags


def half_rows(tile_rows, index, rows, giving):
    block_rows = rows // lax.axis_size("bz")
    half = jnp.bitwise_and(lax.axis_index("bz") + (1 if giving else 0), 1)
    to = pl.multiple_of(index * tile_rows, tile_rows)
    row = (lax.div(to, block_rows) + half) * block_rows + to
    return to, pl.multiple_of(row, tile_rows)


def band_matrix():
    k = jnp.bitwise_and(lax.broadcasted_iota(jnp.int32, (2 * LANES, LANES), 0), LANES - 1)
    gap = k - lax.broadcasted_iota(jnp.int32, (2 * LANES, LANES), 1)
    band = jnp.where(gap == 1, 8.0, jnp.where(gap == -1, -8.0, 0.0))
    band = band + jnp.where(gap == 2, -1.0, jnp.where(gap == -2, 1.0, 0.0))
    return band.astype(jnp.bfloat16)


def slopes_along_y(padded, band, row, planes):
    coarse, fine = [], []
    for z in range(planes):
        plane = padded[REACH + z, pl.ds(PAD + row, TILE), :]
        rounded = plane.astype(jnp.bfloat16)
        coarse.append(rounded)
        fine.append((plane - rounded.astype(jnp.float32)).astype(jnp.bfloat16))
    both = jnp.concatenate([jnp.concatenate(coarse, axis=0), jnp.concatenate(fine, axis=0)], axis=1)
    return jnp.dot(both, band, preferred_element_type=jnp.float32)


def take(tables, first, low, upper):
    found = [
        jnp.take_along_axis(tables[first + k], low, axis=1, mode="promise_in_bounds")
        for k in range(2)
    ]
    return jnp.where(upper, found[1], found[0])


def absorb(padded, material, tables, z, row, clear, scale):
    density = padded[REACH + z, pl.ds(PAD + row, SUBLANES), :]
    label = material[z, pl.ds(row, SUBLANES), :]
    low = jnp.bitwise_and(label, LANES - 1)
    upper = label >= LANES
    rg = take(tables, 0, low, upper)
    be = take(tables, 2, low, upper)
    extinct = jnp.bitwise_and(be, 65535).astype(jnp.float32)
    after = clear * jnp.exp2(extinct * (density * scale))
    stopped = clear - after
    whole = (jnp.right_shift(rg, 16), jnp.bitwise_and(rg, 65535), jnp.right_shift(be, 16))
    return [stopped * part.astype(jnp.float32) for part in whole], after


def shading_at(padded, slope_y, beside, at_edge, z, row):
    at = lambda dz, dx: padded[REACH + z + dz, pl.ds(PAD + row + dx, SUBLANES), :]
    sz = 8.0 * (at(1, 0) - at(-1, 0)) - (at(2, 0) - at(-2, 0))
    sx = 8.0 * (at(0, 1) - at(0, -1)) - (at(0, 2) - at(0, -2))
    outer = pltpu.roll(beside, jnp.bitwise_and(-4 * z - REACH, LANES - 1), 1)
    sy = slope_y + jnp.where(at_edge, outer, 0.0)
    size = sx * sx + sy * sy + sz * sz
    facing = jnp.abs(0.432 * sx + 0.54 * sy + 0.576 * sz)
    return 0.1 + facing * lax.rsqrt(jnp.maximum(size, 36.0))


def edge_lanes():
    lane = lane_index()
    return jnp.logical_or(lane < REACH, lane >= LANES - REACH)


def scale_of(total_planes):
    return -3.0 * math.log2(math.e) / (EXTINCTION_UNIT * total_planes)


def local_give_kernel(total_planes, padded, material, tables, flags, lit, slope_y, through):
    planes, rows, _ = material.shape
    backward = jnp.max(flags[0]) > 0.5
    band = band_matrix()
    scale = scale_of(total_planes)

    def tile(index, carry):
        for step in range(2):
            to, row = half_rows(TILE, 2 * index + step, rows, True)
            slopes = slopes_along_y(padded, band, row, planes)
            for z in range(planes):
                slope_y[z, pl.ds(to, TILE), :] = slopes[TILE * z : TILE * (z + 1)]
            for part in range(0, TILE, SUBLANES):
                clear = jnp.ones((SUBLANES, LANES), jnp.float32)
                for visit in range(planes):
                    z = jnp.where(backward, planes - 1 - visit, visit)
                    light, clear = absorb(padded, material, tables, z, row + part, clear, scale)
                    for c in range(3):
                        lit[c, z, pl.ds(to + part, SUBLANES), :] = light[c]
                through[pl.ds(to + part, SUBLANES), :] = clear
        return carry

    lax.fori_loop(0, rows // 2 // TILE // 2, tile, 0)


def local_give(padded, material, tables, flags, total_planes):
    planes, rows, cols = material.shape
    shape = lambda *dims: pltpu.VMEM(dims, jnp.float32)
    return pl.pallas_call(
        functools.partial(local_give_kernel, total_planes),
        out_shape=(
            shape(3, planes, rows // 2, cols),
            shape(planes, rows // 2, cols),
            shape(rows // 2, cols),
        ),
        in_specs=[VMEM] * 4,
        out_specs=(VMEM,) * 3,
        compiler_params=pltpu.CompilerParams(vmem_limit_bytes=VMEM_LIMIT),
        cost_estimate=pl.CostEstimate(
            flops=20 * planes * rows * cols,
            bytes_accessed=2**22,
            transcendentals=planes * rows * cols,
        ),
        name="local_give",
    )(padded, material, tables, flags)


def put_halo(padded, xa, xb, za, zb, ya, yb, edge, planes, rows):
    odd_x, odd_y, odd_z = is_odd("bx"), is_odd("by"), is_odd("bz")
    for z in range(planes):
        first, second = xa[REACH * z : REACH * (z + 1), :], xb[REACH * z : REACH * (z + 1), :]
        padded[REACH + z, PAD - REACH : PAD, :] = jnp.where(odd_x, first, second)
        padded[REACH + z, PAD + rows : PAD + rows + REACH, :] = jnp.where(odd_x, second, first)
    for layer in range(REACH):
        first = za[layer]
        second = zb[layer] if zb.shape == za.shape else jnp.zeros_like(first)
        padded[layer, PAD : PAD + rows, :] = jnp.where(odd_z, first, second)
        padded[REACH + planes + layer, PAD : PAD + rows, :] = jnp.where(odd_z, second, first)
    side = jnp.bitwise_and(lane_index(), 3)
    for row in range(0, rows, SUBLANES):
        source = row % (rows // 2)
        first, second = ya[source : source + SUBLANES, :], yb[source : source + SUBLANES, :]
        from_low = jnp.where(odd_y, first, second)
        from_high = jnp.where(odd_y, second, first)
        if row >= rows // 2:
            from_low = pltpu.roll(from_low, LANES - 2, 1)
            from_high = pltpu.roll(from_high, 2, 1)
        near = jnp.where(side < 2, from_low, from_high)
        ahead1, ahead2 = pltpu.roll(near, LANES - 1, 1), pltpu.roll(near, LANES - 2, 1)
        behind1, behind2 = pltpu.roll(near, 1, 1), pltpu.roll(near, 2, 1)
        edge[row : row + SUBLANES, :] = jnp.where(
            side == 0,
            -ahead2,
            jnp.where(
                side == 1,
                8.0 * ahead1 - ahead2,
                jnp.where(side == 2, behind2 - 8.0 * behind1, behind2),
            ),
        )


def shade_give_kernel(padded_in, xa, xb, za, zb, ya, yb, lit, slope_y, through, padded, edge, give):
    _, planes, half, _ = lit.shape
    rows = 2 * half
    del padded_in
    put_halo(padded, xa, xb, za, zb, ya, yb, edge, planes, rows)
    at_edge = edge_lanes()

    def tile(index, carry):
        for step in range(2 * (TILE // SUBLANES)):
            to, row = half_rows(TILE, 2 * index + step // 2, rows, True)
            part = step % 2 * SUBLANES
            beside = edge[pl.ds(row + part, SUBLANES), :]
            place = pl.ds(to + part, SUBLANES)
            sums = [jnp.zeros((SUBLANES, LANES), jnp.float32) for _ in range(3)]
            for z in range(planes):
                shading = shading_at(padded, slope_y[z, place, :], beside, at_edge, z, row + part)
                for c in range(3):
                    sums[c] = sums[c] + shading * lit[c, z, place, :]
            for c in range(3):
                give[c, place, :] = sums[c] * (1.0 / COLOR_UNIT)
            give[3, place, :] = through[place, :]
        return carry

    lax.fori_loop(0, half // TILE // 2, tile, 0)


def shade_give(padded, halos, lit, slope_y, through):
    _, _, half, cols = lit.shape
    shape = lambda *dims: pltpu.VMEM(dims, jnp.float32)
    return pl.pallas_call(
        shade_give_kernel,
        out_shape=(shape(*padded.shape), shape(2 * half, LANES), shape(4, half, cols)),
        in_specs=[VMEM] * 10,
        out_specs=(VMEM,) * 3,
        input_output_aliases={0: 0},
        compiler_params=pltpu.CompilerParams(vmem_limit_bytes=VMEM_LIMIT),
        name="shade_give",
    )(padded, *halos, lit, slope_y, through)


def keep_kernel(total_planes, padded, edge, material, tables, flags, keep, slope_y):
    planes, rows, _ = material.shape
    backward = jnp.max(flags[0]) > 0.5
    band = band_matrix()
    scale = scale_of(total_planes)
    at_edge = edge_lanes()

    def tile(index, carry):
        to, row = half_rows(TILE, index, rows, False)
        slope_y[...] = slopes_along_y(padded, band, row, planes).reshape(planes, TILE, LANES)
        for part in range(0, TILE, SUBLANES):
            beside = edge[pl.ds(row + part, SUBLANES), :]
            place = pl.ds(to + part, SUBLANES)
            clear = jnp.ones((SUBLANES, LANES), jnp.float32)
            sums = [jnp.zeros((SUBLANES, LANES), jnp.float32) for _ in range(3)]
            for visit in range(planes):
                z = jnp.where(backward, planes - 1 - visit, visit)
                slope = slope_y[z, part : part + SUBLANES, :]
                light, clear = absorb(padded, material, tables, z, row + part, clear, scale)
                shading = shading_at(padded, slope, beside, at_edge, z, row + part)
                for c in range(3):
                    sums[c] = sums[c] + shading * light[c]
            for c in range(3):
                keep[c, place, :] = sums[c] * (1.0 / COLOR_UNIT)
            keep[3, place, :] = clear
        return carry

    lax.fori_loop(0, rows // 2 // TILE, tile, 0)


def shade_keep(padded, edge, material, tables, flags, total_planes):
    planes, rows, cols = material.shape
    return pl.pallas_call(
        functools.partial(keep_kernel, total_planes),
        out_shape=pltpu.VMEM((4, rows // 2, cols), jnp.float32),
        in_specs=[VMEM] * 5,
        out_specs=VMEM,
        scratch_shapes=[pltpu.VMEM((planes, TILE, LANES), jnp.float32)],
        compiler_params=pltpu.CompilerParams(vmem_limit_bytes=VMEM_LIMIT),
        cost_estimate=pl.CostEstimate(
            flops=40 * planes * rows * cols,
            bytes_accessed=2**22,
            transcendentals=planes * rows * cols,
        ),
        name="keep",
    )(padded, edge, material, tables, flags)


def blend_kernel(bit, last, flags, mine, other, out):
    clear_mine, clear_other = mine[3], other[3]
    behind = jnp.broadcast_to(flags[1 + bit, 0:1, :], clear_mine.shape) > 0.5
    clear = jnp.where(behind, clear_other, clear_mine)
    for c in range(3):
        front = jnp.where(behind, other[c], mine[c])
        back = jnp.where(behind, mine[c], other[c])
        out[c] = front + clear * back
    product = clear_mine * clear_other
    out[3] = 1.0 - product if last else product


def blend(flags, mine, other, bit, last):
    return pl.pallas_call(
        functools.partial(blend_kernel, bit, last),
        out_shape=jax.ShapeDtypeStruct(mine.shape, jnp.float32),
        in_specs=[VMEM] * 3,
        out_specs=VMEM,
        compiler_params=pltpu.CompilerParams(vmem_limit_bytes=VMEM_LIMIT),
        name="blend",
    )(flags, mine, other)


def shards(density, material, color_table, extinction_table, order):
    planes, rows, cols = density.shape
    counts = {axis: lax.axis_size(axis) for axis in ("bx", "by", "bz")}
    slabs = counts["bz"]
    padded, ya, yb, xa, xb, za, zb, tables, flags = faces(
        order, density, color_table, extinction_table, counts
    )
    pairs = {axis: swaps(counts[axis]) for axis in counts}
    xa = lax.ppermute(xa, "bx", pairs["bx"][0])
    xb = lax.ppermute(xb, "bx", pairs["bx"][1])
    za = lax.ppermute(za, "bz", pairs["bz"][0])
    if slabs > 2:
        zb = lax.ppermute(zb, "bz", pairs["bz"][1])
    ya = lax.ppermute(ya, "by", pairs["by"][0])
    yb = lax.ppermute(yb, "by", pairs["by"][1])
    lit, slope_y, through = local_give(padded, material, tables, flags, planes * slabs)
    halos = (xa, xb, za, zb, ya, yb)
    padded, edge, give = shade_give(padded, halos, lit, slope_y, through)
    keep = shade_keep(padded, edge, material, tables, flags, planes * slabs)
    block_rows = rows // slabs
    levels = slabs.bit_length() - 1
    my_slab = lax.axis_index("bz")
    for bit in range(levels):
        flip = [(i, i ^ (1 << bit)) for i in range(slabs)]
        received = lax.ppermute(give, "bz", flip)
        holding = blend(flags, keep, received, bit, bit == levels - 1)
        if bit < levels - 1:
            paired = holding.reshape(4, -1, 2, block_rows, cols)
            half = jnp.bitwise_and(jnp.right_shift(my_slab, bit + 1), 1)
            take = lambda which: lax.dynamic_index_in_dim(paired, which, 2, keepdims=False)
            keep, give = (take(which).reshape(4, -1, cols) for which in (half, 1 - half))
    return holding


def solution(mesh):
    placed = (P("bz", "bx", "by"), P("bz", "bx", "by"), P(), P(), P("bx", "by", None))
    return jax.shard_map(
        shards, mesh=mesh, in_specs=placed, out_specs=P(None, ("bx", "bz"), "by"), check_vma=False
    )
```

```python
import functools
import math

import jax
import jax.numpy as jnp
from jax import lax
from jax.experimental import pallas as pl
from jax.experimental.pallas import tpu as pltpu
from jax.sharding import PartitionSpec as P

LANES = 128
SUBLANES = 8
TILE = 16
PAD = 8
REACH = 2
COLOR_UNIT = 4096.0
EXTINCTION_UNIT = 2048.0
VMEM_LIMIT = 12 * 2**20

VMEM = pl.BlockSpec(memory_space=pltpu.VMEM)
HBM = pl.BlockSpec(memory_space=pltpu.HBM)


def lane_index():
    return lax.broadcasted_iota(jnp.int32, (SUBLANES, LANES), 1)


def is_odd(axis):
    return jnp.bitwise_and(lax.axis_index(axis), 1) == 1


def swaps(count, closed=False):
    first = [(i, i ^ 1) for i in range(count)]
    second = [(i, i + 1 if i % 2 else i - 1) for i in range(1, count - 1)]
    if closed:
        second = [(0, count - 1)] + second + [(count - 1, 0)]
    return first, second


def x_face(out, source, start, planes):
    for z in range(planes):
        out[REACH * z : REACH * (z + 1), :] = source(z, start)


def early_kernel(counts, order, density, colors, extinction, xa, za, zb, tables, flags, place, hues, thick, rows_x, arrived):
    planes, rows, _ = density.shape
    odd_x, odd_z, top = is_odd("bx"), is_odd("bz"), planes - REACH
    ends = [(za, jnp.where(odd_z, 0, top))]
    if counts["bz"] > 2:
        ends.append((zb, jnp.where(odd_z, top, 0)))
    low_x = pl.multiple_of(jnp.where(odd_x, 0, rows - SUBLANES), SUBLANES)
    pairs = [(density.at[:, pl.ds(low_x, SUBLANES), :], rows_x)]
    pairs += [(density.at[pl.ds(start, REACH)], out) for out, start in ends]
    pairs += [(order, place), (colors, hues), (extinction, thick)]
    copies = [
        pltpu.make_async_copy(source, target, arrived.at[k])
        for k, (source, target) in enumerate(pairs)
    ]
    for copy in copies:
        copy.start()
    for copy in copies[-3:]:
        copy.wait()
    slabs = counts["bz"]
    backward = (place[0, 0, 0] > place[0, 0, slabs - 1]).astype(jnp.float32)
    rank = jnp.bitwise_xor(lax.axis_index("bz"), place[0, 0, 0])
    flags[0] = jnp.full((SUBLANES, LANES), backward, jnp.float32)
    for bit in range(slabs.bit_length() - 1):
        behind = jnp.bitwise_and(jnp.right_shift(rank, bit), 1).astype(jnp.float32)
        flags[1 + bit] = jnp.full((SUBLANES, LANES), behind, jnp.float32)
    color = (hues[...].astype(jnp.float32) * COLOR_UNIT).astype(jnp.int32)
    dense = (thick[...].astype(jnp.float32) * EXTINCTION_UNIT).astype(jnp.int32)
    for k, table in enumerate((color[0:1] * 65536 + color[1:2], color[2:3] * 65536 + dense)):
        for part in range(2):
            tables[2 * k + part] = jnp.broadcast_to(
                table[:, part * LANES : (part + 1) * LANES], (SUBLANES, LANES)
            )
    if counts["bz"] == 2:
        zb[...] = jnp.zeros(zb.shape, jnp.float32)
    for copy in copies[:-3]:
        copy.wait()
    start = jnp.where(odd_x, 0, SUBLANES - REACH)
    x_face(xa, lambda z, at: rows_x[z, pl.ds(at, REACH), :], start, planes)


def pack_kernel(density, padded, ya, yb, xb, columns, arrived):
    planes, rows, _ = density.shape
    whole = pltpu.make_async_copy(
        density, padded.at[pl.ds(REACH, planes), pl.ds(PAD, rows), :], arrived
    )
    whole.start()
    start = jnp.where(is_odd("bx"), rows - REACH, 0)
    x_face(xb, lambda z, at: density[z, pl.ds(at, REACH), :], start, planes)
    slot = jnp.right_shift(lane_index(), 2)
    for row in range(0, rows, SUBLANES):
        packed = jnp.zeros((SUBLANES, LANES), jnp.float32)
        for z in range(planes):
            plane = density[z, row : row + SUBLANES, :]
            packed = jnp.where(slot == z, pltpu.roll(plane, (4 * z + REACH) % LANES, 1), packed)
        columns[row : row + SUBLANES, :] = packed
    side = jnp.bitwise_and(lane_index(), 3)
    odd_y = is_odd("by")
    for row in range(0, rows // 2, SUBLANES):
        upper = columns[row : row + SUBLANES, :]
        lower = pltpu.roll(columns[rows // 2 + row : rows // 2 + row + SUBLANES, :], 2, 1)
        high_face = jnp.where(side < 2, upper, lower)
        lower = pltpu.roll(lower, LANES - 4, 1)
        low_face = jnp.where(side < 2, lower, upper)
        ya[row : row + SUBLANES, :] = jnp.where(odd_y, low_face, high_face)
        yb[row : row + SUBLANES, :] = jnp.where(odd_y, high_face, low_face)
    whole.wait()


def faces(order, density, colors, extinction, counts):
    planes, rows, cols = density.shape
    shape = lambda *dims: pltpu.VMEM(dims, jnp.float32)
    z_rows = rows if counts["bz"] > 2 else SUBLANES
    face = REACH * rows
    size = max(REACH * planes, rows // 2)
    params = pltpu.CompilerParams(vmem_limit_bytes=VMEM_LIMIT)
    fixed = [
        pltpu.with_memory_space_constraint(a, pltpu.HBM)
        for a in (order, density, colors, extinction)
    ]
    xa, za, zb, tables, flags = pl.pallas_call(
        functools.partial(early_kernel, counts),
        out_shape=(
            shape(face + 24, cols),
            shape(REACH, rows, cols),
            shape(REACH, z_rows, cols),
            pltpu.VMEM((4, SUBLANES, LANES), jnp.int32),
            shape(counts["bz"].bit_length(), SUBLANES, LANES),
        ),
        in_specs=[HBM] * 4,
        out_specs=(VMEM,) * 5,
        scratch_shapes=[
            pltpu.SMEM(order.shape, jnp.int32),
            pltpu.VMEM(colors.shape, colors.dtype),
            pltpu.VMEM(extinction.shape, extinction.dtype),
            pltpu.VMEM((planes, SUBLANES, cols), jnp.float32),
            pltpu.SemaphoreType.DMA((6,)),
        ],
        compiler_params=params,
        name="early",
    )(*fixed)
    padded, ya, yb, xb = pl.pallas_call(
        pack_kernel,
        out_shape=(
            shape(planes + 2 * REACH, rows + 2 * PAD, cols),
            shape(size + 16, LANES),
            shape(size, LANES),
            shape(size + 8, cols),
        ),
        in_specs=[VMEM],
        out_specs=(VMEM,) * 4,
        scratch_shapes=[pltpu.VMEM((rows, LANES), jnp.float32), pltpu.SemaphoreType.DMA],
        compiler_params=params,
        name="pack",
    )(density)
    return padded, ya, yb, xa, xb, za, zb, tables, flags


def half_rows(tile_rows, index, rows, giving):
    block_rows = rows // lax.axis_size("bz")
    half = jnp.bitwise_and(lax.axis_index("bz") + (1 if giving else 0), 1)
    to = pl.multiple_of(index * tile_rows, tile_rows)
    row = (lax.div(to, block_rows) + half) * block_rows + to
    return to, pl.multiple_of(row, tile_rows)


def band_matrix():
    k = jnp.bitwise_and(lax.broadcasted_iota(jnp.int32, (2 * LANES, LANES), 0), LANES - 1)
    gap = k - lax.broadcasted_iota(jnp.int32, (2 * LANES, LANES), 1)
    band = jnp.where(gap == 1, 8.0, jnp.where(gap == -1, -8.0, 0.0))
    band = band + jnp.where(gap == 2, -1.0, jnp.where(gap == -2, 1.0, 0.0))
    return band.astype(jnp.bfloat16)


def slopes_along_y(padded, band, row, planes):
    coarse, fine = [], []
    for z in range(planes):
        plane = padded[REACH + z, pl.ds(PAD + row, TILE), :]
        rounded = plane.astype(jnp.bfloat16)
        coarse.append(rounded)
        fine.append((plane - rounded.astype(jnp.float32)).astype(jnp.bfloat16))
    both = jnp.concatenate([jnp.concatenate(coarse, axis=0), jnp.concatenate(fine, axis=0)], axis=1)
    return jnp.dot(both, band, preferred_element_type=jnp.float32)


def take(tables, first, low, upper):
    found = [
        jnp.take_along_axis(tables[first + k], low, axis=1, mode="promise_in_bounds")
        for k in range(2)
    ]
    return jnp.where(upper, found[1], found[0])


def absorb(padded, material, tables, z, row, clear, scale):
    density = padded[REACH + z, pl.ds(PAD + row, SUBLANES), :]
    label = material[z, pl.ds(row, SUBLANES), :]
    low = jnp.bitwise_and(label, LANES - 1)
    upper = label >= LANES
    rg = take(tables, 0, low, upper)
    be = take(tables, 2, low, upper)
    extinct = jnp.bitwise_and(be, 65535).astype(jnp.float32)
    after = clear * jnp.exp2(extinct * (density * scale))
    stopped = clear - after
    whole = (jnp.right_shift(rg, 16), jnp.bitwise_and(rg, 65535), jnp.right_shift(be, 16))
    return [stopped * part.astype(jnp.float32) for part in whole], after


def shading_at(padded, slope_y, beside, at_edge, z, row):
    at = lambda dz, dx: padded[REACH + z + dz, pl.ds(PAD + row + dx, SUBLANES), :]
    sz = 8.0 * (at(1, 0) - at(-1, 0)) - (at(2, 0) - at(-2, 0))
    sx = 8.0 * (at(0, 1) - at(0, -1)) - (at(0, 2) - at(0, -2))
    outer = pltpu.roll(beside, jnp.bitwise_and(-4 * z - REACH, LANES - 1), 1)
    sy = slope_y + jnp.where(at_edge, outer, 0.0)
    size = sx * sx + sy * sy + sz * sz
    facing = jnp.abs(0.432 * sx + 0.54 * sy + 0.576 * sz)
    return 0.1 + facing * lax.rsqrt(jnp.maximum(size, 36.0))


def edge_lanes():
    lane = lane_index()
    return jnp.logical_or(lane < REACH, lane >= LANES - REACH)


def scale_of(total_planes):
    return -3.0 * math.log2(math.e) / (EXTINCTION_UNIT * total_planes)


def local_give_kernel(total_planes, padded, material, tables, flags, lit, slope_y, through):
    planes, rows, _ = material.shape
    backward = jnp.max(flags[0]) > 0.5
    band = band_matrix()
    scale = scale_of(total_planes)

    def tile(index, carry):
        for step in range(2):
            to, row = half_rows(TILE, 2 * index + step, rows, True)
            slopes = slopes_along_y(padded, band, row, planes)
            for z in range(planes):
                slope_y[z, pl.ds(to, TILE), :] = slopes[TILE * z : TILE * (z + 1)]
            for part in range(0, TILE, SUBLANES):
                clear = jnp.ones((SUBLANES, LANES), jnp.float32)
                for visit in range(planes):
                    z = jnp.where(backward, planes - 1 - visit, visit)
                    light, clear = absorb(padded, material, tables, z, row + part, clear, scale)
                    for c in range(3):
                        lit[c, z, pl.ds(to + part, SUBLANES), :] = light[c]
                through[pl.ds(to + part, SUBLANES), :] = clear
        return carry

    lax.fori_loop(0, rows // 2 // TILE // 2, tile, 0)


def local_give(padded, material, tables, flags, total_planes):
    planes, rows, cols = material.shape
    shape = lambda *dims: pltpu.VMEM(dims, jnp.float32)
    return pl.pallas_call(
        functools.partial(local_give_kernel, total_planes),
        out_shape=(
            shape(3, planes, rows // 2, cols),
            shape(planes, rows // 2, cols),
            shape(rows // 2, cols),
        ),
        in_specs=[VMEM] * 4,
        out_specs=(VMEM,) * 3,
        compiler_params=pltpu.CompilerParams(vmem_limit_bytes=VMEM_LIMIT),
        cost_estimate=pl.CostEstimate(
            flops=20 * planes * rows * cols,
            bytes_accessed=2**22,
            transcendentals=planes * rows * cols,
        ),
        name="local_give",
    )(padded, material, tables, flags)


def put_halo(padded, xa, xb, za, zb, ya, yb, edge, planes, rows):
    odd_x, odd_y, odd_z = is_odd("bx"), is_odd("by"), is_odd("bz")
    place_x = lax.axis_index("bx")
    end_x = jnp.logical_or(place_x == 0, place_x == lax.axis_size("bx") - 1)
    for z in range(planes):
        first, second = xa[REACH * z : REACH * (z + 1), :], xb[REACH * z : REACH * (z + 1), :]
        second = jnp.where(end_x, 0.0, second)
        padded[REACH + z, PAD - REACH : PAD, :] = jnp.where(odd_x, first, second)
        padded[REACH + z, PAD + rows : PAD + rows + REACH, :] = jnp.where(odd_x, second, first)
    for layer in range(REACH):
        first = za[layer]
        second = zb[layer] if zb.shape == za.shape else jnp.zeros_like(first)
        padded[layer, PAD : PAD + rows, :] = jnp.where(odd_z, first, second)
        padded[REACH + planes + layer, PAD : PAD + rows, :] = jnp.where(odd_z, second, first)
    side = jnp.bitwise_and(lane_index(), 3)
    for row in range(0, rows, SUBLANES):
        source = row % (rows // 2)
        first, second = ya[source : source + SUBLANES, :], yb[source : source + SUBLANES, :]
        from_low = jnp.where(odd_y, first, second)
        from_high = jnp.where(odd_y, second, first)
        if row >= rows // 2:
            from_low = pltpu.roll(from_low, LANES - 2, 1)
            from_high = pltpu.roll(from_high, 2, 1)
        near = jnp.where(side < 2, from_low, from_high)
        ahead1, ahead2 = pltpu.roll(near, LANES - 1, 1), pltpu.roll(near, LANES - 2, 1)
        behind1, behind2 = pltpu.roll(near, 1, 1), pltpu.roll(near, 2, 1)
        edge[row : row + SUBLANES, :] = jnp.where(
            side == 0,
            -ahead2,
            jnp.where(
                side == 1,
                8.0 * ahead1 - ahead2,
                jnp.where(side == 2, behind2 - 8.0 * behind1, behind2),
            ),
        )


def shade_give_kernel(padded_in, xa, xb, za, zb, ya, yb, lit, slope_y, through, padded, edge, give):
    _, planes, half, _ = lit.shape
    rows = 2 * half
    del padded_in
    put_halo(padded, xa, xb, za, zb, ya, yb, edge, planes, rows)
    at_edge = edge_lanes()

    def tile(index, carry):
        for step in range(2 * (TILE // SUBLANES)):
            to, row = half_rows(TILE, 2 * index + step // 2, rows, True)
            part = step % 2 * SUBLANES
            beside = edge[pl.ds(row + part, SUBLANES), :]
            place = pl.ds(to + part, SUBLANES)
            sums = [jnp.zeros((SUBLANES, LANES), jnp.float32) for _ in range(3)]
            for z in range(planes):
                shading = shading_at(padded, slope_y[z, place, :], beside, at_edge, z, row + part)
                for c in range(3):
                    sums[c] = sums[c] + shading * lit[c, z, place, :]
            for c in range(3):
                give[c, place, :] = sums[c] * (1.0 / COLOR_UNIT)
            give[3, place, :] = through[place, :]
        return carry

    lax.fori_loop(0, half // TILE // 2, tile, 0)


def shade_give(padded, halos, lit, slope_y, through):
    _, _, half, cols = lit.shape
    shape = lambda *dims: pltpu.VMEM(dims, jnp.float32)
    return pl.pallas_call(
        shade_give_kernel,
        out_shape=(shape(*padded.shape), shape(2 * half, LANES), shape(4, half, cols)),
        in_specs=[VMEM] * 10,
        out_specs=(VMEM,) * 3,
        input_output_aliases={0: 0},
        compiler_params=pltpu.CompilerParams(vmem_limit_bytes=VMEM_LIMIT),
        name="shade_give",
    )(padded, *halos, lit, slope_y, through)


def keep_kernel(total_planes, padded, edge, material, tables, flags, keep, slope_y):
    planes, rows, _ = material.shape
    backward = jnp.max(flags[0]) > 0.5
    band = band_matrix()
    scale = scale_of(total_planes)
    at_edge = edge_lanes()

    def tile(index, carry):
        to, row = half_rows(TILE, index, rows, False)
        slope_y[...] = slopes_along_y(padded, band, row, planes).reshape(planes, TILE, LANES)
        for part in range(0, TILE, SUBLANES):
            beside = edge[pl.ds(row + part, SUBLANES), :]
            place = pl.ds(to + part, SUBLANES)
            clear = jnp.ones((SUBLANES, LANES), jnp.float32)
            sums = [jnp.zeros((SUBLANES, LANES), jnp.float32) for _ in range(3)]
            for visit in range(planes):
                z = jnp.where(backward, planes - 1 - visit, visit)
                slope = slope_y[z, part : part + SUBLANES, :]
                light, clear = absorb(padded, material, tables, z, row + part, clear, scale)
                shading = shading_at(padded, slope, beside, at_edge, z, row + part)
                for c in range(3):
                    sums[c] = sums[c] + shading * light[c]
            for c in range(3):
                keep[c, place, :] = sums[c] * (1.0 / COLOR_UNIT)
            keep[3, place, :] = clear
        return carry

    lax.fori_loop(0, rows // 2 // TILE, tile, 0)


def shade_keep(padded, edge, material, tables, flags, total_planes):
    planes, rows, cols = material.shape
    return pl.pallas_call(
        functools.partial(keep_kernel, total_planes),
        out_shape=pltpu.VMEM((4, rows // 2, cols), jnp.float32),
        in_specs=[VMEM] * 5,
        out_specs=VMEM,
        scratch_shapes=[pltpu.VMEM((planes, TILE, LANES), jnp.float32)],
        compiler_params=pltpu.CompilerParams(vmem_limit_bytes=VMEM_LIMIT),
        cost_estimate=pl.CostEstimate(
            flops=40 * planes * rows * cols,
            bytes_accessed=2**22,
            transcendentals=planes * rows * cols,
        ),
        name="keep",
    )(padded, edge, material, tables, flags)


def blend_kernel(bit, last, flags, mine, other, out):
    clear_mine, clear_other = mine[3], other[3]
    behind = jnp.broadcast_to(flags[1 + bit, 0:1, :], clear_mine.shape) > 0.5
    clear = jnp.where(behind, clear_other, clear_mine)
    for c in range(3):
        front = jnp.where(behind, other[c], mine[c])
        back = jnp.where(behind, mine[c], other[c])
        out[c] = front + clear * back
    product = clear_mine * clear_other
    out[3] = 1.0 - product if last else product


def blend(flags, mine, other, bit, last):
    return pl.pallas_call(
        functools.partial(blend_kernel, bit, last),
        out_shape=jax.ShapeDtypeStruct(mine.shape, jnp.float32),
        in_specs=[VMEM] * 3,
        out_specs=VMEM,
        compiler_params=pltpu.CompilerParams(vmem_limit_bytes=VMEM_LIMIT),
        name="blend",
    )(flags, mine, other)


def shards(density, material, color_table, extinction_table, order):
    planes, rows, cols = density.shape
    counts = {axis: lax.axis_size(axis) for axis in ("bx", "by", "bz")}
    slabs = counts["bz"]
    padded, ya, yb, xa, xb, za, zb, tables, flags = faces(
        order, density, color_table, extinction_table, counts
    )
    pairs = {axis: swaps(counts[axis], axis == "bx") for axis in counts}
    xa = lax.ppermute(xa, "bx", pairs["bx"][0])
    xb = lax.ppermute(xb, "bx", pairs["bx"][1])
    za = lax.ppermute(za, "bz", pairs["bz"][0])
    if slabs > 2:
        zb = lax.ppermute(zb, "bz", pairs["bz"][1])
    ya = lax.ppermute(ya, "by", pairs["by"][0])
    yb = lax.ppermute(yb, "by", pairs["by"][1])
    lit, slope_y, through = local_give(padded, material, tables, flags, planes * slabs)
    halos = (xa, xb, za, zb, ya, yb)
    padded, edge, give = shade_give(padded, halos, lit, slope_y, through)
    keep = shade_keep(padded, edge, material, tables, flags, planes * slabs)
    block_rows = rows // slabs
    levels = slabs.bit_length() - 1
    my_slab = lax.axis_index("bz")
    for bit in range(levels):
        flip = [(i, i ^ (1 << bit)) for i in range(slabs)]
        received = lax.ppermute(give, "bz", flip)
        holding = blend(flags, keep, received, bit, bit == levels - 1)
        if bit < levels - 1:
            paired = holding.reshape(4, -1, 2, block_rows, cols)
            half = jnp.bitwise_and(jnp.right_shift(my_slab, bit + 1), 1)
            take = lambda which: lax.dynamic_index_in_dim(paired, which, 2, keepdims=False)
            keep, give = (take(which).reshape(4, -1, cols) for which in (half, 1 - half))
    return holding


def solution(mesh):
    placed = (P("bz", "bx", "by"), P("bz", "bx", "by"), P(), P(), P("bx", "by", None))
    return jax.shard_map(
        shards, mesh=mesh, in_specs=placed, out_specs=P(None, ("bx", "bz"), "by"), check_vma=False
    )
```

```python
import functools
import math

import jax
import jax.numpy as jnp
from jax import lax
from jax.experimental import pallas as pl
from jax.experimental.pallas import tpu as pltpu
from jax.sharding import PartitionSpec as P

LANES = 128
SUBLANES = 8
TILE = 16
PAD = 8
REACH = 2
COLOR_UNIT = 4096.0
EXTINCTION_UNIT = 2048.0
VMEM_LIMIT = 12 * 2**20

VMEM = pl.BlockSpec(memory_space=pltpu.VMEM)
HBM = pl.BlockSpec(memory_space=pltpu.HBM)


def lane_index():
    return lax.broadcasted_iota(jnp.int32, (SUBLANES, LANES), 1)


def is_odd(axis):
    return jnp.bitwise_and(lax.axis_index(axis), 1) == 1


def swaps(count, closed=False):
    first = [(i, i ^ 1) for i in range(count)]
    second = [(i, i + 1 if i % 2 else i - 1) for i in range(1, count - 1)]
    if closed:
        second = [(0, count - 1)] + second + [(count - 1, 0)]
    return first, second


def x_face(out, source, start, planes):
    for z in range(planes):
        out[REACH * z : REACH * (z + 1), :] = source(z, start)


def early_kernel(counts, order, density, colors, extinction, xa, za, zb, tables, flags, place, hues, thick, rows_x, arrived):
    planes, rows, _ = density.shape
    odd_x, odd_z, top = is_odd("bx"), is_odd("bz"), planes - REACH
    ends = [(za, jnp.where(odd_z, 0, top))]
    if counts["bz"] > 2:
        ends.append((zb, jnp.where(odd_z, top, 0)))
    low_x = pl.multiple_of(jnp.where(odd_x, 0, rows - SUBLANES), SUBLANES)
    pairs = [(density.at[:, pl.ds(low_x, SUBLANES), :], rows_x)]
    pairs += [(density.at[pl.ds(start, REACH)], out) for out, start in ends]
    pairs += [(order, place), (colors, hues), (extinction, thick)]
    copies = [
        pltpu.make_async_copy(source, target, arrived.at[k])
        for k, (source, target) in enumerate(pairs)
    ]
    for copy in copies:
        copy.start()
    for copy in copies[-3:]:
        copy.wait()
    slabs = counts["bz"]
    backward = (place[0, 0, 0] > place[0, 0, slabs - 1]).astype(jnp.float32)
    rank = jnp.bitwise_xor(lax.axis_index("bz"), place[0, 0, 0])
    flags[0] = jnp.full((SUBLANES, LANES), backward, jnp.float32)
    for bit in range(slabs.bit_length() - 1):
        behind = jnp.bitwise_and(jnp.right_shift(rank, bit), 1).astype(jnp.float32)
        flags[1 + bit] = jnp.full((SUBLANES, LANES), behind, jnp.float32)
    color = (hues[...].astype(jnp.float32) * COLOR_UNIT).astype(jnp.int32)
    dense = (thick[...].astype(jnp.float32) * EXTINCTION_UNIT).astype(jnp.int32)
    for k, table in enumerate((color[0:1] * 65536 + color[1:2], color[2:3] * 65536 + dense)):
        for part in range(2):
            tables[2 * k + part] = jnp.broadcast_to(
                table[:, part * LANES : (part + 1) * LANES], (SUBLANES, LANES)
            )
    if counts["bz"] == 2:
        zb[...] = jnp.zeros(zb.shape, jnp.float32)
    for copy in copies[:-3]:
        copy.wait()
    start = jnp.where(odd_x, 0, SUBLANES - REACH)
    x_face(xa, lambda z, at: rows_x[z, pl.ds(at, REACH), :], start, planes)


def pack_kernel(density, padded, ya, yb, xb, columns, arrived):
    planes, rows, _ = density.shape
    whole = pltpu.make_async_copy(
        density, padded.at[pl.ds(REACH, planes), pl.ds(PAD, rows), :], arrived
    )
    whole.start()
    start = jnp.where(is_odd("bx"), rows - REACH, 0)
    x_face(xb, lambda z, at: density[z, pl.ds(at, REACH), :], start, planes)
    slot = jnp.right_shift(lane_index(), 2)
    for row in range(0, rows, SUBLANES):
        packed = jnp.zeros((SUBLANES, LANES), jnp.float32)
        for z in range(planes):
            plane = density[z, row : row + SUBLANES, :]
            packed = jnp.where(slot == z, pltpu.roll(plane, (4 * z + REACH) % LANES, 1), packed)
        columns[row : row + SUBLANES, :] = packed
    side = jnp.bitwise_and(lane_index(), 3)
    odd_y = is_odd("by")
    for row in range(0, rows // 2, SUBLANES):
        upper = columns[row : row + SUBLANES, :]
        lower = pltpu.roll(columns[rows // 2 + row : rows // 2 + row + SUBLANES, :], 2, 1)
        high_face = jnp.where(side < 2, upper, lower)
        lower = pltpu.roll(lower, LANES - 4, 1)
        low_face = jnp.where(side < 2, lower, upper)
        ya[row : row + SUBLANES, :] = jnp.where(odd_y, low_face, high_face)
        yb[row : row + SUBLANES, :] = jnp.where(odd_y, high_face, low_face)
    whole.wait()


def faces(order, density, colors, extinction, counts):
    planes, rows, cols = density.shape
    shape = lambda *dims: pltpu.VMEM(dims, jnp.float32)
    z_rows = rows if counts["bz"] > 2 else SUBLANES
    face = REACH * rows
    size = max(REACH * planes, rows // 2)
    params = pltpu.CompilerParams(vmem_limit_bytes=VMEM_LIMIT)
    fixed = [
        pltpu.with_memory_space_constraint(a, pltpu.HBM)
        for a in (order, density, colors, extinction)
    ]
    xa, za, zb, tables, flags = pl.pallas_call(
        functools.partial(early_kernel, counts),
        out_shape=(
            shape(face + 24, cols),
            shape(REACH, rows, cols),
            shape(REACH, z_rows, cols),
            pltpu.VMEM((4, SUBLANES, LANES), jnp.int32),
            shape(counts["bz"].bit_length(), SUBLANES, LANES),
        ),
        in_specs=[HBM] * 4,
        out_specs=(VMEM,) * 5,
        scratch_shapes=[
            pltpu.SMEM(order.shape, jnp.int32),
            pltpu.VMEM(colors.shape, colors.dtype),
            pltpu.VMEM(extinction.shape, extinction.dtype),
            pltpu.VMEM((planes, SUBLANES, cols), jnp.float32),
            pltpu.SemaphoreType.DMA((6,)),
        ],
        compiler_params=params,
        name="early",
    )(*fixed)
    padded, ya, yb, xb = pl.pallas_call(
        pack_kernel,
        out_shape=(
            shape(planes + 2 * REACH, rows + 2 * PAD, cols),
            shape(size + 16, LANES),
            shape(size, LANES),
            shape(size + 24, cols),
        ),
        in_specs=[VMEM],
        out_specs=(VMEM,) * 4,
        scratch_shapes=[pltpu.VMEM((rows, LANES), jnp.float32), pltpu.SemaphoreType.DMA],
        compiler_params=params,
        name="pack",
    )(density)
    return padded, ya, yb, xa, xb, za, zb, tables, flags


def half_rows(tile_rows, index, rows, giving):
    block_rows = rows // lax.axis_size("bz")
    half = jnp.bitwise_and(lax.axis_index("bz") + (1 if giving else 0), 1)
    to = pl.multiple_of(index * tile_rows, tile_rows)
    row = (lax.div(to, block_rows) + half) * block_rows + to
    return to, pl.multiple_of(row, tile_rows)


def band_matrix():
    k = jnp.bitwise_and(lax.broadcasted_iota(jnp.int32, (2 * LANES, LANES), 0), LANES - 1)
    gap = k - lax.broadcasted_iota(jnp.int32, (2 * LANES, LANES), 1)
    band = jnp.where(gap == 1, 8.0, jnp.where(gap == -1, -8.0, 0.0))
    band = band + jnp.where(gap == 2, -1.0, jnp.where(gap == -2, 1.0, 0.0))
    return band.astype(jnp.bfloat16)


def slopes_along_y(padded, band, row, planes):
    coarse, fine = [], []
    for z in range(planes):
        plane = padded[REACH + z, pl.ds(PAD + row, TILE), :]
        rounded = plane.astype(jnp.bfloat16)
        coarse.append(rounded)
        fine.append((plane - rounded.astype(jnp.float32)).astype(jnp.bfloat16))
    both = jnp.concatenate([jnp.concatenate(coarse, axis=0), jnp.concatenate(fine, axis=0)], axis=1)
    return jnp.dot(both, band, preferred_element_type=jnp.float32)


def take(tables, first, low, upper):
    found = [
        jnp.take_along_axis(tables[first + k], low, axis=1, mode="promise_in_bounds")
        for k in range(2)
    ]
    return jnp.where(upper, found[1], found[0])


def absorb(padded, material, tables, z, row, clear, scale):
    density = padded[REACH + z, pl.ds(PAD + row, SUBLANES), :]
    label = material[z, pl.ds(row, SUBLANES), :]
    low = jnp.bitwise_and(label, LANES - 1)
    upper = label >= LANES
    rg = take(tables, 0, low, upper)
    be = take(tables, 2, low, upper)
    extinct = jnp.bitwise_and(be, 65535).astype(jnp.float32)
    after = clear * jnp.exp2(extinct * (density * scale))
    stopped = clear - after
    whole = (jnp.right_shift(rg, 16), jnp.bitwise_and(rg, 65535), jnp.right_shift(be, 16))
    return [stopped * part.astype(jnp.float32) for part in whole], after


def shading_at(padded, slope_y, beside, at_edge, z, row):
    at = lambda dz, dx: padded[REACH + z + dz, pl.ds(PAD + row + dx, SUBLANES), :]
    sz = 8.0 * (at(1, 0) - at(-1, 0)) - (at(2, 0) - at(-2, 0))
    sx = 8.0 * (at(0, 1) - at(0, -1)) - (at(0, 2) - at(0, -2))
    outer = pltpu.roll(beside, jnp.bitwise_and(-4 * z - REACH, LANES - 1), 1)
    sy = slope_y + jnp.where(at_edge, outer, 0.0)
    size = sx * sx + sy * sy + sz * sz
    facing = jnp.abs(0.432 * sx + 0.54 * sy + 0.576 * sz)
    return 0.1 + facing * lax.rsqrt(jnp.maximum(size, 36.0))


def edge_lanes():
    lane = lane_index()
    return jnp.logical_or(lane < REACH, lane >= LANES - REACH)


def scale_of(total_planes):
    return -3.0 * math.log2(math.e) / (EXTINCTION_UNIT * total_planes)


def local_give_kernel(total_planes, padded, material, tables, flags, lit, slope_y, through):
    planes, rows, _ = material.shape
    backward = jnp.max(flags[0]) > 0.5
    band = band_matrix()
    scale = scale_of(total_planes)

    def tile(index, carry):
        for step in range(2):
            to, row = half_rows(TILE, 2 * index + step, rows, True)
            slopes = slopes_along_y(padded, band, row, planes)
            for z in range(planes):
                slope_y[z, pl.ds(to, TILE), :] = slopes[TILE * z : TILE * (z + 1)]
            for part in range(0, TILE, SUBLANES):
                clear = jnp.ones((SUBLANES, LANES), jnp.float32)
                for visit in range(planes):
                    z = jnp.where(backward, planes - 1 - visit, visit)
                    light, clear = absorb(padded, material, tables, z, row + part, clear, scale)
                    for c in range(3):
                        lit[c, z, pl.ds(to + part, SUBLANES), :] = light[c]
                through[pl.ds(to + part, SUBLANES), :] = clear
        return carry

    lax.fori_loop(0, rows // 2 // TILE // 2, tile, 0)


def local_give(padded, material, tables, flags, total_planes):
    planes, rows, cols = material.shape
    shape = lambda *dims: pltpu.VMEM(dims, jnp.float32)
    return pl.pallas_call(
        functools.partial(local_give_kernel, total_planes),
        out_shape=(
            shape(3, planes, rows // 2, cols),
            shape(planes, rows // 2, cols),
            shape(rows // 2, cols),
        ),
        in_specs=[VMEM] * 4,
        out_specs=(VMEM,) * 3,
        compiler_params=pltpu.CompilerParams(vmem_limit_bytes=VMEM_LIMIT),
        cost_estimate=pl.CostEstimate(
            flops=20 * planes * rows * cols,
            bytes_accessed=2**22,
            transcendentals=planes * rows * cols,
        ),
        name="local_give",
    )(padded, material, tables, flags)


def put_halo(padded, xa, xb, za, zb, ya, yb, edge, planes, rows):
    odd_x, odd_y, odd_z = is_odd("bx"), is_odd("by"), is_odd("bz")
    place_x = lax.axis_index("bx")
    end_x = jnp.logical_or(place_x == 0, place_x == lax.axis_size("bx") - 1)
    for z in range(planes):
        first, second = xa[REACH * z : REACH * (z + 1), :], xb[REACH * z : REACH * (z + 1), :]
        second = jnp.where(end_x, 0.0, second)
        padded[REACH + z, PAD - REACH : PAD, :] = jnp.where(odd_x, first, second)
        padded[REACH + z, PAD + rows : PAD + rows + REACH, :] = jnp.where(odd_x, second, first)
    for layer in range(REACH):
        first = za[layer]
        second = zb[layer] if zb.shape == za.shape else jnp.zeros_like(first)
        padded[layer, PAD : PAD + rows, :] = jnp.where(odd_z, first, second)
        padded[REACH + planes + layer, PAD : PAD + rows, :] = jnp.where(odd_z, second, first)
    side = jnp.bitwise_and(lane_index(), 3)
    for row in range(0, rows, SUBLANES):
        source = row % (rows // 2)
        first, second = ya[source : source + SUBLANES, :], yb[source : source + SUBLANES, :]
        from_low = jnp.where(odd_y, first, second)
        from_high = jnp.where(odd_y, second, first)
        if row >= rows // 2:
            from_low = pltpu.roll(from_low, LANES - 2, 1)
            from_high = pltpu.roll(from_high, 2, 1)
        near = jnp.where(side < 2, from_low, from_high)
        ahead1, ahead2 = pltpu.roll(near, LANES - 1, 1), pltpu.roll(near, LANES - 2, 1)
        behind1, behind2 = pltpu.roll(near, 1, 1), pltpu.roll(near, 2, 1)
        edge[row : row + SUBLANES, :] = jnp.where(
            side == 0,
            -ahead2,
            jnp.where(
                side == 1,
                8.0 * ahead1 - ahead2,
                jnp.where(side == 2, behind2 - 8.0 * behind1, behind2),
            ),
        )


def shade_give_kernel(padded_in, xa, xb, za, zb, ya, yb, lit, slope_y, through, padded, edge, give):
    _, planes, half, _ = lit.shape
    rows = 2 * half
    del padded_in
    put_halo(padded, xa, xb, za, zb, ya, yb, edge, planes, rows)
    at_edge = edge_lanes()

    def tile(index, carry):
        for step in range(2 * (TILE // SUBLANES)):
            to, row = half_rows(TILE, 2 * index + step // 2, rows, True)
            part = step % 2 * SUBLANES
            beside = edge[pl.ds(row + part, SUBLANES), :]
            place = pl.ds(to + part, SUBLANES)
            sums = [jnp.zeros((SUBLANES, LANES), jnp.float32) for _ in range(3)]
            for z in range(planes):
                shading = shading_at(padded, slope_y[z, place, :], beside, at_edge, z, row + part)
                for c in range(3):
                    sums[c] = sums[c] + shading * lit[c, z, place, :]
            for c in range(3):
                give[c, place, :] = sums[c] * (1.0 / COLOR_UNIT)
            give[3, place, :] = through[place, :]
        return carry

    lax.fori_loop(0, half // TILE // 2, tile, 0)


def shade_give(padded, halos, lit, slope_y, through):
    _, _, half, cols = lit.shape
    shape = lambda *dims: pltpu.VMEM(dims, jnp.float32)
    return pl.pallas_call(
        shade_give_kernel,
        out_shape=(shape(*padded.shape), shape(2 * half, LANES), shape(4, half, cols)),
        in_specs=[VMEM] * 10,
        out_specs=(VMEM,) * 3,
        input_output_aliases={0: 0},
        compiler_params=pltpu.CompilerParams(vmem_limit_bytes=VMEM_LIMIT),
        name="shade_give",
    )(padded, *halos, lit, slope_y, through)


def keep_kernel(total_planes, padded, edge, material, tables, flags, keep, slope_y):
    planes, rows, _ = material.shape
    backward = jnp.max(flags[0]) > 0.5
    band = band_matrix()
    scale = scale_of(total_planes)
    at_edge = edge_lanes()

    def tile(index, carry):
        to, row = half_rows(TILE, index, rows, False)
        slope_y[...] = slopes_along_y(padded, band, row, planes).reshape(planes, TILE, LANES)
        for part in range(0, TILE, SUBLANES):
            beside = edge[pl.ds(row + part, SUBLANES), :]
            place = pl.ds(to + part, SUBLANES)
            clear = jnp.ones((SUBLANES, LANES), jnp.float32)
            sums = [jnp.zeros((SUBLANES, LANES), jnp.float32) for _ in range(3)]
            for visit in range(planes):
                z = jnp.where(backward, planes - 1 - visit, visit)
                slope = slope_y[z, part : part + SUBLANES, :]
                light, clear = absorb(padded, material, tables, z, row + part, clear, scale)
                shading = shading_at(padded, slope, beside, at_edge, z, row + part)
                for c in range(3):
                    sums[c] = sums[c] + shading * light[c]
            for c in range(3):
                keep[c, place, :] = sums[c] * (1.0 / COLOR_UNIT)
            keep[3, place, :] = clear
        return carry

    lax.fori_loop(0, rows // 2 // TILE, tile, 0)


def shade_keep(padded, edge, material, tables, flags, total_planes):
    planes, rows, cols = material.shape
    return pl.pallas_call(
        functools.partial(keep_kernel, total_planes),
        out_shape=pltpu.VMEM((4, rows // 2, cols), jnp.float32),
        in_specs=[VMEM] * 5,
        out_specs=VMEM,
        scratch_shapes=[pltpu.VMEM((planes, TILE, LANES), jnp.float32)],
        compiler_params=pltpu.CompilerParams(vmem_limit_bytes=VMEM_LIMIT),
        cost_estimate=pl.CostEstimate(
            flops=40 * planes * rows * cols,
            bytes_accessed=2**22,
            transcendentals=planes * rows * cols,
        ),
        name="keep",
    )(padded, edge, material, tables, flags)


def blend_kernel(bit, last, flags, mine, other, out):
    clear_mine, clear_other = mine[3], other[3]
    behind = jnp.broadcast_to(flags[1 + bit, 0:1, :], clear_mine.shape) > 0.5
    clear = jnp.where(behind, clear_other, clear_mine)
    for c in range(3):
        front = jnp.where(behind, other[c], mine[c])
        back = jnp.where(behind, mine[c], other[c])
        out[c] = front + clear * back
    product = clear_mine * clear_other
    out[3] = 1.0 - product if last else product


def blend(flags, mine, other, bit, last):
    return pl.pallas_call(
        functools.partial(blend_kernel, bit, last),
        out_shape=jax.ShapeDtypeStruct(mine.shape, jnp.float32),
        in_specs=[VMEM] * 3,
        out_specs=VMEM,
        compiler_params=pltpu.CompilerParams(vmem_limit_bytes=VMEM_LIMIT),
        name="blend",
    )(flags, mine, other)


def shards(density, material, color_table, extinction_table, order):
    planes, rows, cols = density.shape
    counts = {axis: lax.axis_size(axis) for axis in ("bx", "by", "bz")}
    slabs = counts["bz"]
    padded, ya, yb, xa, xb, za, zb, tables, flags = faces(
        order, density, color_table, extinction_table, counts
    )
    pairs = {axis: swaps(counts[axis], axis == "bx") for axis in counts}
    xa = lax.ppermute(xa, "bx", pairs["bx"][0])
    xb = lax.ppermute(xb, "bx", pairs["bx"][1])
    za = lax.ppermute(za, "bz", pairs["bz"][0])
    if slabs > 2:
        zb = lax.ppermute(zb, "bz", pairs["bz"][1])
    ya = lax.ppermute(ya, "by", pairs["by"][0])
    yb = lax.ppermute(yb, "by", pairs["by"][1])
    lit, slope_y, through = local_give(padded, material, tables, flags, planes * slabs)
    halos = (xa, xb, za, zb, ya, yb)
    padded, edge, give = shade_give(padded, halos, lit, slope_y, through)
    keep = shade_keep(padded, edge, material, tables, flags, planes * slabs)
    block_rows = rows // slabs
    levels = slabs.bit_length() - 1
    my_slab = lax.axis_index("bz")
    for bit in range(levels):
        flip = [(i, i ^ (1 << bit)) for i in range(slabs)]
        received = lax.ppermute(give, "bz", flip)
        holding = blend(flags, keep, received, bit, bit == levels - 1)
        if bit < levels - 1:
            paired = holding.reshape(4, -1, 2, block_rows, cols)
            half = jnp.bitwise_and(jnp.right_shift(my_slab, bit + 1), 1)
            take = lambda which: lax.dynamic_index_in_dim(paired, which, 2, keepdims=False)
            keep, give = (take(which).reshape(4, -1, cols) for which in (half, 1 - half))
    return holding


def solution(mesh):
    placed = (P("bz", "bx", "by"), P("bz", "bx", "by"), P(), P(), P("bx", "by", None))
    return jax.shard_map(
        shards, mesh=mesh, in_specs=placed, out_specs=P(None, ("bx", "bz"), "by"), check_vma=False
    )
```
